32 devices in a mesh: groups: 2 (over x), tm: 16 (over z, y, core).
Axes of the slice: x: 2, y: 2, z: 4, core: 2. Of those that a mesh axis runs over, the one named last changes fastest.
Arguments:
- tokens: bfloat16 [2, 4096, 1152], P('groups', 'tm'), parts along dimension 0, may hold values from -6 to 6
- norm_gain: float32 [1152], replicated, may hold values from 0.5 to 8
- w_qkv: bfloat16 [1152, 1728], P('tm'), may hold values from -0.1875 to 0.1875
- w_out: bfloat16 [1152, 576], P('tm'), may hold values from -0.25 to 0.25
- block_mask: int32 [2, 2, 2], P('groups'), parts along dimension 0, may hold values from 0 to 1
- keep_tiles: int32 [2, 256], P('groups', 'tm'), parts along dimension 0, may hold values 0 or 1
- cotangent: bfloat16 [2, 4096, 1152], P('groups', 'tm'), parts along dimension 0, may hold values from -6 to 6
Outputs:
- mixed: bfloat16 [2, 4096, 1152], P('groups', 'tm'), parts along dimension 0
- grad_tokens: bfloat16 [2, 4096, 1152], P('groups', 'tm'), parts along dimension 0
- grad_qkv: float32 [2304, 1728], P(('groups', 'tm')), parts along dimension 0
- grad_out: float32 [2304, 576], P(('groups', 'tm')), parts along dimension 0
The draws below stay inside these ranges and needn't reach their ends.
There are 2 independent parts, one for each index of `groups`. The reference program is written for one: setup_inputs(seed, part) draws one part's arguments, and reference() takes and returns one part's arrays. A program takes and returns all parts, laid end to end along the dimension named above; an argument that names none is the same for every part. Nothing has to cross between parts.
All inputs are finite; a program needn't handle non-finite values. No bound on the sum of `keep_tiles` on one device may be relied on, other than what follows from the above.
Results may differ from the reference program's by a relative error of at most 0.0055.
The reference program's roundings to bfloat16 on the way (of `hidden`, `qkv`, `d_attn`, `probs_b`, `attn`, `dscore`, `d_qkv` and `d_hidden`) count: a program that leaves them out, or rounds other values in their place, can miss the bound.
Values may be sent and summed in bfloat16 or wider, within the bound.
A program may use at most 128 MiB of HBM per device.

```python
import jax
import jax.numpy as jnp
from jax import lax

D = 1152
HEADS = 8
HD = 72
PATCHES = 1024
TB = 2
TILE = 16
VIDEOS = 1
E = 576
FRAMES = 4
TOKENS = 4096
FB = 2


def draw_norm_gain(key, part):
    return jax.random.uniform(key, (D,), jnp.float32, 0.5, 1.5)


def place_ends(drawn, rng, low, top_value):
    spot = [jax.random.randint(jax.random.fold_in(rng, axis), (), 0, length) for axis, length in enumerate(drawn.shape)]
    widest = drawn.shape.index(max(drawn.shape))
    beside = spot[:widest] + [(spot[widest] + 1) % drawn.shape[widest]] + spot[widest + 1:]
    return drawn.at[tuple(spot)].set(low).at[tuple(beside)].set(top_value)


def raised(drawn, own_key, source, target, shards_of, factor):
    owner, partner = [(jnp.arange(drawn.shape[dim]) // (drawn.shape[dim] // shards_of)).reshape([-1 if axis == dim else 1 for axis in range(drawn.ndim)]) for dim in (source, target)]
    chosen = jax.random.permutation(own_key, shards_of)[partner]
    strong = (owner == chosen) | (owner == (partner + shards_of // 2) % shards_of)
    return jnp.where(strong, factor * drawn, drawn)


def shard_levels(stream_key, dims, split, least, high):
    def one(axis_at, parts):
        draws = jax.random.uniform(jax.random.fold_in(jax.random.fold_in(stream_key, 6), axis_at), (parts,), jnp.float32, least / len(split), high / len(split))
        return jnp.repeat(jnp.exp(draws), dims[axis_at] // parts).reshape((-1,) + (1,) * (len(dims) - axis_at - 1))

    factor_of = one(*split[0])
    for cut in split[1:]:
        factor_of = factor_of * one(*cut)
    return factor_of


def scatter_about(key, shape, spread, limit, cuts=(), dtype=jnp.bfloat16):
    drawn = spread * jax.random.normal(key, shape, jnp.float32)
    if cuts:
        drawn = drawn * shard_levels(key, shape, cuts, -0.22, 0.18)
    return jnp.clip(drawn, -limit, limit).astype(dtype)


def heavy_noise(key, shape, scale, reach, split, heavy, dtype=jnp.bfloat16):
    values = scale * jax.random.normal(key, shape, jnp.float32)
    if split:
        values = values * shard_levels(key, shape, split, -0.22, 0.18)
    return jnp.clip(raised(values, jax.random.fold_in(key, 3), *heavy), -reach, reach).astype(dtype)


def setup_inputs(seed: int = 0, part: int = 0) -> dict:
    seeds = jax.random.split(jax.random.key(seed), 8)
    own_keys = jax.random.split(jax.random.fold_in(seeds[7], part), 8)
    tokens = scatter_about(own_keys[0], (VIDEOS, TOKENS, D), 1.0, 6.0, ((1, 16),))
    norm_gain = draw_norm_gain(jax.random.fold_in(seeds[7], 71), part)
    w_qkv = scatter_about(seeds[2], (D, 3 * E), D ** -0.5, 0.1875, ((0, 16),))
    w_out = scatter_about(seeds[3], (D, E), E ** -0.5, 0.25, ((0, 16),))
    block_mask = place_ends(jax.random.randint(own_keys[4], (VIDEOS, FB, FB), 0, 2), jax.random.fold_in(own_keys[4], 1), 0, 1).astype(jnp.int32)
    keep_tiles = place_ends((jax.random.randint(own_keys[5], (VIDEOS, TOKENS // TILE), 0, 4) < 3).astype(jnp.int32), jax.random.fold_in(own_keys[5], 1), 0, 1)
    cotangent = heavy_noise(own_keys[6], (VIDEOS, TOKENS, D), 1.0, 6.0, ((1, 16),), (1, 2, 16, 2.0))
    return dict(tokens=tokens, norm_gain=norm_gain, w_qkv=w_qkv, w_out=w_out, block_mask=block_mask, keep_tiles=keep_tiles, cotangent=cotangent)


EPS = 1e-06

def reference(tokens, norm_gain, w_qkv, w_out, block_mask, keep_tiles, cotangent):
    frame_block = jnp.arange(FRAMES) // TB
    scale = HD ** (-0.5)

    def per_video(carry, item):
        tok_in, grad_in, blk, keep = item
        tok_float = tok_in.astype(jnp.float32)
        inv_rms = lax.rsqrt(lax.optimization_barrier(jnp.mean(tok_float * tok_float, -1, keepdims=True)) + EPS)
        normed = tok_float * inv_rms
        hidden = (normed * norm_gain).astype(jnp.bfloat16)
        qkv = jnp.dot(hidden, w_qkv, preferred_element_type=jnp.float32).astype(jnp.bfloat16)
        qkv = qkv.reshape(FRAMES, PATCHES, 3, HEADS, HD)
        d_attn = jnp.dot(grad_in, w_out, preferred_element_type=jnp.float32).astype(jnp.bfloat16)
        d_out = d_attn.reshape(FRAMES, PATCHES, HEADS, HD).astype(jnp.float32)
        blocks = jnp.repeat(jnp.repeat(blk, TB, 0), TB, 1) > 0
        same_block = frame_block[:, None] == frame_block[None, :]
        block_allow = blocks | same_block
        kept = jnp.repeat(keep, TILE).reshape(FRAMES, PATCHES) > 0
        diag_one = jnp.arange(FRAMES)[:, None] == jnp.arange(FRAMES)[None, :]
        allow = (block_allow[None] & (kept.T[:, None, :] | diag_one[None]))[:, None]
        queries = qkv[:, :, 0].astype(jnp.float32)
        key_part = qkv[:, :, 1].astype(jnp.float32)
        val_part = qkv[:, :, 2].astype(jnp.float32)
        scores = jnp.einsum('fphd,gphd->phfg', queries, key_part) * scale
        scores = jnp.where(allow, scores, -1e+30)
        row_top = lax.optimization_barrier(jnp.max(scores, -1, keepdims=True))
        expo = jnp.exp(scores - row_top)
        probs = expo / lax.optimization_barrier(jnp.sum(expo, -1, keepdims=True))
        probs_b = probs.astype(jnp.bfloat16).astype(jnp.float32)
        attn = jnp.einsum('phfg,gphd->fphd', probs_b, val_part).astype(jnp.bfloat16)
        dprob = jnp.einsum('fphd,gphd->phfg', d_out, val_part)
        dscore = probs * (dprob - lax.optimization_barrier(jnp.sum(probs * dprob, -1, keepdims=True)))
        dscore_b = dscore.astype(jnp.bfloat16).astype(jnp.float32)
        grad_query = (jnp.einsum('phfg,gphd->fphd', dscore_b, key_part) * scale).astype(jnp.bfloat16)
        grad_key = (jnp.einsum('phfg,fphd->gphd', dscore_b, queries) * scale).astype(jnp.bfloat16)
        grad_value = jnp.einsum('phfg,fphd->gphd', probs_b, d_out).astype(jnp.bfloat16)
        d_qkv = jnp.stack([grad_query, grad_key, grad_value], axis=2).reshape(TOKENS, 3 * E)
        attn = attn.reshape(TOKENS, E)
        mixed = (tok_float + jnp.dot(attn, w_out.T, preferred_element_type=jnp.float32)).astype(jnp.bfloat16)
        part_out = jnp.dot(grad_in.T, attn, preferred_element_type=jnp.float32)
        part_qkv = jnp.dot(hidden.T, d_qkv, preferred_element_type=jnp.float32)
        d_hidden = lax.optimization_barrier(jnp.dot(d_qkv, w_qkv.T, preferred_element_type=jnp.float32).astype(jnp.bfloat16))
        grad = d_hidden.astype(jnp.float32) * norm_gain
        grad_tok = grad_in.astype(jnp.float32) + inv_rms * (grad - normed * lax.optimization_barrier(jnp.mean(grad * normed, -1, keepdims=True)))
        return ((carry[0] + part_qkv, carry[1] + part_out), (mixed, grad_tok.astype(jnp.bfloat16)))
    start = (jnp.zeros((D, 3 * E), jnp.float32), jnp.zeros((D, E), jnp.float32))
    totals, outs = lax.scan(per_video, start, (tokens, cotangent, block_mask, keep_tiles))
    return (outs[0], outs[1], totals[0], totals[1])
```

```python
import functools

import jax
import jax.numpy as jnp
from jax import lax
from jax.experimental import pallas as pl
from jax.experimental.pallas import tpu as pltpu
from jax.sharding import PartitionSpec as P

HD = 72
SPLIT = 4
TB = 2
TILE = 16


EPS = 1e-06
FRAMES_HERE = 4
MESH = pl.DeviceIdType.MESH


def temporal(qkv_cols, dattn_cols, keep_cols, block_mask, frames):
    videos, per_owner, owners, _ = qkv_cols.shape
    band_count = owners // frames
    heads_n = dattn_cols.shape[-1] // HD
    scale = HD ** (-0.5)
    parts = qkv_cols.reshape(videos, per_owner, frames, band_count, 3, heads_n, HD)
    queries = parts[:, :, :, :, 0]
    key_part = parts[:, :, :, :, 1]
    val_part = parts[:, :, :, :, 2]
    d_out = dattn_cols.reshape(videos, per_owner, frames, band_count, heads_n, HD)
    frame_block = jnp.arange(frames) // TB
    blocks = jnp.repeat(jnp.repeat(block_mask, TB, 1), TB, 2) > 0
    same_block = frame_block[:, None] == frame_block[None, :]
    block_allow = blocks | same_block[None]
    kept = jnp.transpose(keep_cols.reshape(videos, per_owner, frames, band_count) > 0, (0, 1, 3, 2))
    diag_one = jnp.arange(frames)[:, None] == jnp.arange(frames)[None, :]
    allow = block_allow[:, None, None, None, :, :] & (kept[:, :, :, None, None, :] | diag_one)
    scores = (
        jnp.einsum("vrfshd,vrgshd->vrshfg", queries, key_part, preferred_element_type=jnp.float32)
        * scale
    )
    scores = jnp.where(allow, scores, -1e30)
    row_top = jnp.max(scores, -1, keepdims=True)
    expo = jnp.exp(scores - row_top)
    probs = expo / jnp.sum(expo, -1, keepdims=True)
    probs_b = probs.astype(jnp.bfloat16)
    attn = jnp.einsum(
        "vrshfg,vrgshd->vrfshd", probs_b, val_part, preferred_element_type=jnp.float32
    ).astype(jnp.bfloat16)
    dprob = jnp.einsum("vrfshd,vrgshd->vrshfg", d_out, val_part, preferred_element_type=jnp.float32)
    dscore = probs * (dprob - jnp.sum(probs * dprob, -1, keepdims=True))
    dscore_b = dscore.astype(jnp.bfloat16)
    grad_query = (
        jnp.einsum("vrshfg,vrgshd->vrfshd", dscore_b, key_part, preferred_element_type=jnp.float32)
        * scale
    ).astype(jnp.bfloat16)
    grad_key = (
        jnp.einsum("vrshfg,vrfshd->vrgshd", dscore_b, queries, preferred_element_type=jnp.float32)
        * scale
    ).astype(jnp.bfloat16)
    grad_value = jnp.einsum(
        "vrshfg,vrfshd->vrgshd", probs_b, d_out, preferred_element_type=jnp.float32
    ).astype(jnp.bfloat16)
    d_qkv = jnp.stack([grad_query, grad_key, grad_value], axis=4).reshape(
        videos, per_owner, owners, -1
    )
    return (attn.reshape(videos, per_owner, owners, -1), d_qkv)


def per_device(tokens, norm_gain, w_qkv, w_out, block_mask, keep_tiles, cotangent):
    owners = lax.axis_size("tm")
    videos, band_len, model_width = tokens.shape
    per_owner = band_len // owners
    frames = owners // SPLIT
    qkv_full, out_full = (
        lax.all_gather(w_qkv, "tm", axis=0, tiled=True),
        lax.all_gather(w_out, "tm", axis=0, tiled=True),
    )
    tok_float = tokens.astype(jnp.float32)
    inv_rms = lax.rsqrt(jnp.mean(tok_float * tok_float, -1, keepdims=True) + EPS)
    normed = tok_float * inv_rms
    hidden = (normed * norm_gain).astype(jnp.bfloat16)
    keep_tok = jnp.repeat(keep_tiles, TILE, axis=1).reshape(videos, per_owner, owners)
    qkv = jnp.dot(hidden, qkv_full, preferred_element_type=jnp.float32).astype(jnp.bfloat16)
    d_attn = jnp.dot(cotangent, out_full, preferred_element_type=jnp.float32).astype(jnp.bfloat16)
    qkv_cols, dattn_cols, keep_cols = (
        lax.all_to_all(
            qkv.reshape(videos, per_owner, owners, -1),
            "tm",
            split_axis=2,
            concat_axis=2,
            tiled=True,
        ),
        lax.all_to_all(
            d_attn.reshape(videos, per_owner, owners, -1),
            "tm",
            split_axis=2,
            concat_axis=2,
            tiled=True,
        ),
        lax.all_to_all(keep_tok, "tm", split_axis=2, concat_axis=2, tiled=True),
    )
    attn_cols, dqkv_cols = temporal(qkv_cols, dattn_cols, keep_cols, block_mask, frames)
    attn_rows, dqkv_rows = (
        lax.all_to_all(attn_cols, "tm", split_axis=2, concat_axis=2, tiled=True),
        lax.all_to_all(dqkv_cols, "tm", split_axis=2, concat_axis=2, tiled=True),
    )
    attn = attn_rows.reshape(videos, band_len, -1)
    d_qkv = dqkv_rows.reshape(videos, band_len, -1)
    part_qkv = jnp.einsum("vtd,vte->de", hidden, d_qkv, preferred_element_type=jnp.float32)
    part_out = jnp.einsum("vtd,vte->de", cotangent, attn, preferred_element_type=jnp.float32)
    d_hidden = lax.optimization_barrier(
        jnp.einsum("vte,de->vtd", d_qkv, qkv_full, preferred_element_type=jnp.float32).astype(
            jnp.bfloat16
        )
    )
    grad_qkv, grad_out = (
        lax.psum_scatter(part_qkv, "tm", scatter_dimension=0, tiled=True),
        lax.psum_scatter(part_out, "tm", scatter_dimension=0, tiled=True),
    )
    mixed = (
        tok_float + jnp.einsum("vte,de->vtd", attn, out_full, preferred_element_type=jnp.float32)
    ).astype(jnp.bfloat16)
    grad = d_hidden.astype(jnp.float32) * norm_gain
    grad_tokens = cotangent.astype(jnp.float32) + inv_rms * (
        grad - normed * jnp.mean(grad * normed, -1, keepdims=True)
    )
    return (mixed, grad_tokens.astype(jnp.bfloat16), grad_qkv, grad_out)


def pid(x):
    return {"tm": x}


def place():
    me = lax.axis_index("tm")
    z, b = me // SPLIT, me % SPLIT
    return me, z, b, b // 2, b % 2


def greet(peers):
    barrier = pltpu.get_barrier_semaphore()
    for peer in peers:
        pl.semaphore_signal(barrier, inc=1, device_id=peer, device_id_type=MESH)
    pl.semaphore_wait(barrier, len(peers))


def remote(src, dst, send_sem, recv_sem, peer):
    return pltpu.make_async_remote_copy(
        src_ref=src,
        dst_ref=dst,
        send_sem=send_sem,
        recv_sem=recv_sem,
        device_id=peer,
        device_id_type=MESH,
    )


def gather_kernel(w_ref, out_ref, local_sem, send_z, send_y, send_x, send_c, recv):
    x = lax.axis_index("groups")
    me, z, b, y, c = place()
    over_z = [pid((z + dz) % FRAMES_HERE * SPLIT + b) for dz in range(1, FRAMES_HERE)]
    over_y = pid(z * SPLIT + (1 - y) * 2 + c)
    over_c = pid(z * SPLIT + y * 2 + (1 - c))
    over_x = {"groups": 1 - x}
    greet(over_z + [over_y, over_c, over_x])
    mine = (x, 2)
    started = []

    def send(src, t, k, sem, peer):
        copy = remote(src, out_ref.at[t, k], sem, recv.at[t, k], peer)
        copy.start()
        started.append(copy)

    def arrived(t, k, peer):
        remote(out_ref.at[t, k], out_ref.at[t, k], send_z.at[0, 0], recv.at[t, k], peer).wait_recv()

    local = [
        pltpu.make_async_copy(w_ref.at[t], out_ref.at[t, me], local_sem.at[i])
        for i, t in enumerate(mine)
    ]
    for copy in local:
        copy.start()
    for dz in range(1, FRAMES_HERE):
        for i, t in enumerate(mine):
            send(w_ref.at[t], t, me, send_z.at[i, dz], over_z[dz - 1])
    shards = [(z + FRAMES_HERE - dz) % FRAMES_HERE * SPLIT for dz in range(FRAMES_HERE)]
    order = [0, 1, 3, 2]
    for dz in order:
        k = shards[dz] + b
        for i, t in enumerate(mine):
            if dz:
                arrived(t, k, over_y)
            src = out_ref.at[t, k] if dz else w_ref.at[t]
            send(src, t, k, send_y.at[i, dz], over_y)
            if i == 0:
                send(src, t, k, send_x.at[0, dz], over_x)
            send(src, t, k, send_c.at[i, 0, dz], over_c)
    for dz in order:
        k = shards[dz] + (1 - y) * 2 + c
        for i, t in enumerate(mine):
            arrived(t, k, over_y)
            if i == 0:
                send(out_ref.at[t, k], t, k, send_x.at[1, dz], over_x)
            send(out_ref.at[t, k], t, k, send_c.at[i, 1, dz], over_c)
    for j in range(2):
        for dz in order:
            k = shards[dz] + (y if j == 0 else 1 - y) * 2 + c
            arrived(1 - x, k, over_x)
            send(out_ref.at[1 - x, k], 1 - x, k, send_c.at[2, j, dz], over_c)
    for t in range(3):
        for yy in range(2):
            for zz in range(FRAMES_HERE):
                arrived(t, zz * SPLIT + yy * 2 + (1 - c), over_c)
    for copy in local:
        copy.wait()
    for copy in started:
        copy.wait_send()


def gather_weights(blocks):
    owners = FRAMES_HERE * SPLIT
    dma = pltpu.SemaphoreType.DMA
    return pl.pallas_call(
        gather_kernel,
        out_shape=jax.ShapeDtypeStruct((3, owners) + blocks.shape[1:], blocks.dtype),
        in_specs=[pl.BlockSpec(memory_space=pl.ANY)],
        out_specs=pl.BlockSpec(memory_space=pl.ANY),
        scratch_shapes=[
            dma((2,)),
            dma((2, FRAMES_HERE)),
            dma((2, FRAMES_HERE)),
            dma((2, FRAMES_HERE)),
            dma((3, 2, FRAMES_HERE)),
            dma((3, owners)),
        ],
        compiler_params=pltpu.CompilerParams(collective_id=0, has_side_effects=True),
    )(blocks)


def forward_kernel(
    pay, keep, cols, pay_out, keep_out, cols_out, local_sem, send_z, recv_z, send_b, recv_b
):
    me, z, b, y, c = place()
    over_z = [pid((z + dz) % FRAMES_HERE * SPLIT + b) for dz in range(1, FRAMES_HERE)]
    over_b = [pid(z * SPLIT + (b + db) % SPLIT) for db in range(1, SPLIT)]
    greet(over_z + over_b)
    local = [
        pltpu.make_async_copy(pay.at[z], pay_out.at[z], local_sem.at[0]),
        pltpu.make_async_copy(keep.at[z], keep_out.at[z], local_sem.at[1]),
        pltpu.make_async_copy(cols.at[b], cols_out.at[b], local_sem.at[2]),
    ]
    copies = []
    for dz in (2, 1, 3):
        to = (z + dz) % FRAMES_HERE
        peer = over_z[dz - 1]
        copies.append(remote(keep.at[to], keep_out.at[z], send_z.at[1, dz], recv_z.at[1, dz], peer))
        copies.append(remote(pay.at[to], pay_out.at[z], send_z.at[0, dz], recv_z.at[0, dz], peer))
    for db in (2, 1, 3):
        to = (b + db) % SPLIT
        copies.append(
            remote(cols.at[to], cols_out.at[b], send_b.at[db], recv_b.at[db], over_b[db - 1])
        )
    for copy in copies + local:
        copy.start()
    for dz in (1, 2, 3):
        came = (z + FRAMES_HERE - dz) % FRAMES_HERE
        peer = over_z[dz - 1]
        remote(keep.at[z], keep_out.at[came], send_z.at[1, dz], recv_z.at[1, dz], peer).wait_recv()
        remote(pay.at[z], pay_out.at[came], send_z.at[0, dz], recv_z.at[0, dz], peer).wait_recv()
    for db in (1, 2, 3):
        came = (b + SPLIT - db) % SPLIT
        remote(cols.at[b], cols_out.at[came], send_b.at[db], recv_b.at[db], over_b[db - 1]).wait_recv()
    for copy in local:
        copy.wait()
    for copy in copies:
        copy.wait_send()


def send_forward(pay, keep, cols):
    dma = pltpu.SemaphoreType.DMA
    return pl.pallas_call(
        forward_kernel,
        out_shape=[jax.ShapeDtypeStruct(a.shape, a.dtype) for a in (pay, keep, cols)],
        in_specs=[pl.BlockSpec(memory_space=pl.ANY)] * 3,
        out_specs=[pl.BlockSpec(memory_space=pl.ANY)] * 3,
        scratch_shapes=[dma((3,)), dma((2, 4)), dma((2, 4)), dma((4,)), dma((4,))],
        compiler_params=pltpu.CompilerParams(collective_id=1, has_side_effects=True),
    )(pay, keep, cols)


def back_kernel(res, out, local_sem, send_z, send_y, send_c, recv):
    me, z, b, y, c = place()
    over_z = [pid((z + dz) % FRAMES_HERE * SPLIT + b) for dz in range(1, FRAMES_HERE)]
    over_y = pid(z * SPLIT + (1 - y) * 2 + c)
    over_c = pid(z * SPLIT + y * 2 + (1 - c))
    greet(over_z + [over_y, over_c])
    started = []

    def send(src, i, j, sem, peer):
        copy = remote(src, out.at[i, j], sem, recv.at[i, j], peer)
        copy.start()
        started.append(copy)

    def arrived(i, j, peer):
        remote(out.at[i, j], out.at[i, j], send_z.at[0], recv.at[i, j], peer).wait_recv()

    local = pltpu.make_async_copy(res.at[z], out.at[b, z], local_sem)
    local.start()
    for dz in (2, 1, 3):
        send(res.at[(z + dz) % FRAMES_HERE], b, z, send_z.at[dz], over_z[dz - 1])
    order = [0, 1, 3, 2]
    for dz in order:
        j = (z + FRAMES_HERE - dz) % FRAMES_HERE
        if dz:
            arrived(b, j, over_y)
        src = out.at[b, j] if dz else res.at[z]
        send(src, b, j, send_y.at[dz], over_y)
        send(src, b, j, send_c.at[0, dz], over_c)
    for dz in order:
        i, j = (1 - y) * 2 + c, (z + FRAMES_HERE - dz) % FRAMES_HERE
        arrived(i, j, over_y)
        send(out.at[i, j], i, j, send_c.at[1, dz], over_c)
    for yy in range(2):
        for j in range(FRAMES_HERE):
            arrived(yy * 2 + (1 - c), j, over_c)
    local.wait()
    for copy in started:
        copy.wait_send()


def send_back(res):
    dma = pltpu.SemaphoreType.DMA
    return pl.pallas_call(
        back_kernel,
        out_shape=jax.ShapeDtypeStruct((SPLIT,) + res.shape, res.dtype),
        in_specs=[pl.BlockSpec(memory_space=pl.ANY)],
        out_specs=pl.BlockSpec(memory_space=pl.ANY),
        scratch_shapes=[dma, dma((4,)), dma((4,)), dma((2, 4)), dma((4, 4))],
        compiler_params=pltpu.CompilerParams(collective_id=2, has_side_effects=True),
    )(res)


def sums_kernel(part, out, local_sem, send_z, recv_z):
    me, z, b, y, c = place()
    over_z = [pid((z + dz) % FRAMES_HERE * SPLIT + b) for dz in range(1, FRAMES_HERE)]
    greet(over_z)
    local = pltpu.make_async_copy(part.at[z], out.at[z], local_sem)
    copies = [
        remote(
            part.at[(z + dz) % FRAMES_HERE],
            out.at[z],
            send_z.at[dz],
            recv_z.at[dz],
            over_z[dz - 1],
        )
        for dz in (2, 1, 3)
    ]
    for copy in copies + [local]:
        copy.start()
    for dz in (1, 2, 3):
        came = (z + FRAMES_HERE - dz) % FRAMES_HERE
        remote(part.at[z], out.at[came], send_z.at[dz], recv_z.at[dz], over_z[dz - 1]).wait_recv()
    local.wait()
    for copy in copies:
        copy.wait_send()


def send_sums(part):
    dma = pltpu.SemaphoreType.DMA
    return pl.pallas_call(
        sums_kernel,
        out_shape=jax.ShapeDtypeStruct(part.shape, part.dtype),
        in_specs=[pl.BlockSpec(memory_space=pl.ANY)],
        out_specs=pl.BlockSpec(memory_space=pl.ANY),
        scratch_shapes=[dma, dma((4,)), dma((4,))],
        compiler_params=pltpu.CompilerParams(collective_id=3, has_side_effects=True),
    )(part)


def attention_kernel(pay, allow, out, dk_sum, dv_sum):
    f32, bf16 = jnp.float32, jnp.bfloat16
    width = pay.shape[-1] // 4
    rows = pay.shape[1]
    scale = HD ** (-0.5)
    frames = pay.shape[0]
    row = lax.broadcasted_iota(jnp.int32, (width, 128), 0)
    lane = lax.broadcasted_iota(jnp.int32, (width, 128), 1)
    gather = ((row >= lane * HD) & (row < lane * HD + HD)).astype(f32).astype(bf16)
    row_t = lax.broadcasted_iota(jnp.int32, (128, width), 1)
    lane_t = lax.broadcasted_iota(jnp.int32, (128, width), 0)
    spread = ((row_t >= lane_t * HD) & (row_t < lane_t * HD + HD)).astype(f32).astype(bf16)

    def part(i, f):
        return pay[f, :, i * width : (i + 1) * width].astype(f32)

    def head_sums(prod):
        high = prod.astype(bf16)
        low = (prod - high.astype(f32)).astype(bf16)
        return jnp.dot(high, gather, preferred_element_type=f32) + jnp.dot(
            low, gather, preferred_element_type=f32
        )

    for f in range(frames):
        query, d_out = part(0, f), part(3, f)
        scores, dprob = [], []
        for g in range(frames):
            raw = head_sums(query * part(1, g)) * scale
            scores.append(jnp.where(allow[f * frames + g] > 0, raw, -1e30))
            dprob.append(head_sums(d_out * part(2, g)))
        top = functools.reduce(jnp.maximum, scores)
        expo = [jnp.exp(s - top) for s in scores]
        total = functools.reduce(jnp.add, expo)
        probs = [e / total for e in expo]
        inner = functools.reduce(jnp.add, [p * d for p, d in zip(probs, dprob)])
        attn = jnp.zeros((rows, width), f32)
        d_query = jnp.zeros((rows, width), f32)
        for g in range(frames):
            pb = jnp.dot(probs[g].astype(bf16), spread, preferred_element_type=f32)
            dscore = (probs[g] * (dprob[g] - inner)).astype(bf16)
            ds = jnp.dot(dscore, spread, preferred_element_type=f32)
            attn += pb * part(2, g)
            d_query += ds * part(1, g)
            if f == 0:
                dk_sum[g] = ds * query
                dv_sum[g] = pb * d_out
            else:
                dk_sum[g] += ds * query
                dv_sum[g] += pb * d_out
        out[f, :, 0:width] = attn.astype(bf16)
        out[f, :, width : 2 * width] = (d_query * scale).astype(bf16)
    for g in range(frames):
        out[g, :, 2 * width : 3 * width] = (dk_sum[g] * scale).astype(bf16)
        out[g, :, 3 * width : 4 * width] = dv_sum[g].astype(bf16)


def attention(pay, allow):
    frames, rows, wide = pay.shape
    return pl.pallas_call(
        attention_kernel,
        out_shape=jax.ShapeDtypeStruct(pay.shape, pay.dtype),
        in_specs=[pl.BlockSpec(memory_space=pltpu.VMEM)] * 2,
        out_specs=pl.BlockSpec(memory_space=pltpu.VMEM),
        scratch_shapes=[pltpu.VMEM((frames, rows, wide // 4), jnp.float32)] * 2,
        compiler_params=pltpu.CompilerParams(vmem_limit_bytes=32 * 1024 * 1024),
    )(pay, allow)


def four_frames(tokens, norm_gain, w_qkv, w_out, block_mask, keep_tiles, cotangent):
    f32, bf16 = jnp.float32, jnp.bfloat16
    frames = FRAMES_HERE
    tokens, cotangent = tokens[0], cotangent[0]
    band, model = tokens.shape
    shard, wide_qkv = w_qkv.shape
    wide = wide_qkv + w_out.shape[1]
    rows = band // frames
    blocks = jnp.concatenate([w_qkv, w_out], 1).reshape(shard, 3, wide // 3).transpose(1, 0, 2)
    weights = gather_weights(blocks)
    weights = weights.transpose(1, 2, 0, 3).reshape(model, wide)
    qkv_full, out_full = weights[:, :wide_qkv], weights[:, wide_qkv:]

    tok_float = tokens.astype(f32)
    inv_rms = lax.rsqrt(jnp.mean(tok_float * tok_float, -1, keepdims=True) + EPS)
    normed = tok_float * inv_rms
    hidden = (normed * norm_gain).astype(bf16)
    qkv = jnp.dot(hidden, qkv_full, preferred_element_type=f32).astype(bf16)
    d_attn = jnp.dot(cotangent, out_full, preferred_element_type=f32).astype(bf16)
    pay = jnp.concatenate([qkv, d_attn], 1).reshape(frames, rows, wide)
    keep = jnp.repeat(keep_tiles[0].astype(f32), TILE).reshape(frames, 1, rows)
    keep = jnp.pad(jnp.broadcast_to(keep, (frames, 8, rows)), ((0, 0), (0, 0), (0, 128 - rows)))

    def owners_columns(a):
        return a.reshape(band, frames, SPLIT, shard).transpose(2, 0, 1, 3).reshape(SPLIT, band, -1)

    cols = jnp.concatenate([owners_columns(hidden), owners_columns(cotangent)], 2)
    pay_at, keep_at, cols_at = send_forward(pay, keep, cols)

    frame_block = jnp.arange(frames) // TB
    same_block = frame_block[:, None] == frame_block[None, :]
    seen = (jnp.repeat(jnp.repeat(block_mask[0], TB, 0), TB, 1) > 0) | same_block
    diag_one = jnp.arange(frames)[:, None] == jnp.arange(frames)[None, :]
    kept = keep_at[:, 0, :rows] > 0
    allow = seen[:, :, None] & (kept[None] | diag_one[:, :, None])
    allow = jnp.broadcast_to(
        allow.reshape(frames * frames, rows, 1).astype(f32), (frames * frames, rows, 128)
    )
    res = send_back(attention(pay_at, allow))

    res_all = res.reshape(SPLIT * band, wide)
    width = wide // 4
    mine = lax.dynamic_index_in_dim(res, lax.axis_index("tm") % SPLIT, 0, keepdims=False)
    mine = mine.reshape(band, wide)
    attn, d_qkv = mine[:, :width], mine[:, width:]
    cols_all = cols_at.reshape(SPLIT * band, -1)
    half = cols_all.shape[1] // 2
    part_qkv = jnp.einsum(
        "td,te->de", cols_all[:, :half], res_all[:, width:], preferred_element_type=f32
    )
    part_out = jnp.einsum(
        "td,te->de", cols_all[:, half:], res_all[:, :width], preferred_element_type=f32
    )
    parts = jnp.concatenate([part_qkv, part_out], 1).reshape(frames, shard, wide)
    sums = jnp.sum(send_sums(parts), 0)
    grad_qkv, grad_out = sums[:, :wide_qkv], sums[:, wide_qkv:]

    d_hidden = lax.optimization_barrier(
        jnp.einsum("te,de->td", d_qkv, qkv_full, preferred_element_type=f32).astype(bf16)
    )
    mixed = (
        tok_float + jnp.einsum("te,de->td", attn, out_full, preferred_element_type=f32)
    ).astype(bf16)
    grad = d_hidden.astype(f32) * norm_gain
    grad_tokens = cotangent.astype(f32) + inv_rms * (
        grad - normed * jnp.mean(grad * normed, -1, keepdims=True)
    )
    return (mixed[None], grad_tokens.astype(bf16)[None], grad_qkv, grad_out)


def solution(mesh):
    placed = (
        P("groups", "tm", None),
        P(),
        P("tm", None),
        P("tm", None),
        P("groups", None, None),
        P("groups", "tm"),
        P("groups", "tm", None),
    )
    small = mesh.shape["tm"] == FRAMES_HERE * SPLIT and mesh.shape["groups"] == 2
    return jax.shard_map(
        four_frames if small else per_device,
        mesh=mesh,
        in_specs=placed,
        out_specs=(
            P("groups", "tm", None),
            P("groups", "tm", None),
            P(("groups", "tm"), None),
            P(("groups", "tm"), None),
        ),
        check_vma=False,
    )
```

```python
import functools

import jax
import jax.numpy as jnp
from jax import lax
from jax.experimental import pallas as pl
from jax.experimental.pallas import tpu as pltpu
from jax.sharding import PartitionSpec as P

HD = 72
SPLIT = 4
TB = 2
TILE = 16


EPS = 1e-06
FRAMES_HERE = 4
BLOCK = 768
MESH = pl.DeviceIdType.MESH


def temporal(qkv_cols, dattn_cols, keep_cols, block_mask, frames):
    videos, per_owner, owners, _ = qkv_cols.shape
    band_count = owners // frames
    heads_n = dattn_cols.shape[-1] // HD
    scale = HD ** (-0.5)
    parts = qkv_cols.reshape(videos, per_owner, frames, band_count, 3, heads_n, HD)
    queries = parts[:, :, :, :, 0]
    key_part = parts[:, :, :, :, 1]
    val_part = parts[:, :, :, :, 2]
    d_out = dattn_cols.reshape(videos, per_owner, frames, band_count, heads_n, HD)
    frame_block = jnp.arange(frames) // TB
    blocks = jnp.repeat(jnp.repeat(block_mask, TB, 1), TB, 2) > 0
    same_block = frame_block[:, None] == frame_block[None, :]
    block_allow = blocks | same_block[None]
    kept = jnp.transpose(keep_cols.reshape(videos, per_owner, frames, band_count) > 0, (0, 1, 3, 2))
    diag_one = jnp.arange(frames)[:, None] == jnp.arange(frames)[None, :]
    allow = block_allow[:, None, None, None, :, :] & (kept[:, :, :, None, None, :] | diag_one)
    scores = (
        jnp.einsum("vrfshd,vrgshd->vrshfg", queries, key_part, preferred_element_type=jnp.float32)
        * scale
    )
    scores = jnp.where(allow, scores, -1e30)
    row_top = jnp.max(scores, -1, keepdims=True)
    expo = jnp.exp(scores - row_top)
    probs = expo / jnp.sum(expo, -1, keepdims=True)
    probs_b = probs.astype(jnp.bfloat16)
    attn = jnp.einsum(
        "vrshfg,vrgshd->vrfshd", probs_b, val_part, preferred_element_type=jnp.float32
    ).astype(jnp.bfloat16)
    dprob = jnp.einsum("vrfshd,vrgshd->vrshfg", d_out, val_part, preferred_element_type=jnp.float32)
    dscore = probs * (dprob - jnp.sum(probs * dprob, -1, keepdims=True))
    dscore_b = dscore.astype(jnp.bfloat16)
    grad_query = (
        jnp.einsum("vrshfg,vrgshd->vrfshd", dscore_b, key_part, preferred_element_type=jnp.float32)
        * scale
    ).astype(jnp.bfloat16)
    grad_key = (
        jnp.einsum("vrshfg,vrfshd->vrgshd", dscore_b, queries, preferred_element_type=jnp.float32)
        * scale
    ).astype(jnp.bfloat16)
    grad_value = jnp.einsum(
        "vrshfg,vrfshd->vrgshd", probs_b, d_out, preferred_element_type=jnp.float32
    ).astype(jnp.bfloat16)
    d_qkv = jnp.stack([grad_query, grad_key, grad_value], axis=4).reshape(
        videos, per_owner, owners, -1
    )
    return (attn.reshape(videos, per_owner, owners, -1), d_qkv)


def per_device(tokens, norm_gain, w_qkv, w_out, block_mask, keep_tiles, cotangent):
    owners = lax.axis_size("tm")
    videos, band_len, model_width = tokens.shape
    per_owner = band_len // owners
    frames = owners // SPLIT
    qkv_full, out_full = (
        lax.all_gather(w_qkv, "tm", axis=0, tiled=True),
        lax.all_gather(w_out, "tm", axis=0, tiled=True),
    )
    tok_float = tokens.astype(jnp.float32)
    inv_rms = lax.rsqrt(jnp.mean(tok_float * tok_float, -1, keepdims=True) + EPS)
    normed = tok_float * inv_rms
    hidden = (normed * norm_gain).astype(jnp.bfloat16)
    keep_tok = jnp.repeat(keep_tiles, TILE, axis=1).reshape(videos, per_owner, owners)
    qkv = jnp.dot(hidden, qkv_full, preferred_element_type=jnp.float32).astype(jnp.bfloat16)
    d_attn = jnp.dot(cotangent, out_full, preferred_element_type=jnp.float32).astype(jnp.bfloat16)
    qkv_cols, dattn_cols, keep_cols = (
        lax.all_to_all(
            qkv.reshape(videos, per_owner, owners, -1),
            "tm",
            split_axis=2,
            concat_axis=2,
            tiled=True,
        ),
        lax.all_to_all(
            d_attn.reshape(videos, per_owner, owners, -1),
            "tm",
            split_axis=2,
            concat_axis=2,
            tiled=True,
        ),
        lax.all_to_all(keep_tok, "tm", split_axis=2, concat_axis=2, tiled=True),
    )
    attn_cols, dqkv_cols = temporal(qkv_cols, dattn_cols, keep_cols, block_mask, frames)
    attn_rows, dqkv_rows = (
        lax.all_to_all(attn_cols, "tm", split_axis=2, concat_axis=2, tiled=True),
        lax.all_to_all(dqkv_cols, "tm", split_axis=2, concat_axis=2, tiled=True),
    )
    attn = attn_rows.reshape(videos, band_len, -1)
    d_qkv = dqkv_rows.reshape(videos, band_len, -1)
    part_qkv = jnp.einsum("vtd,vte->de", hidden, d_qkv, preferred_element_type=jnp.float32)
    part_out = jnp.einsum("vtd,vte->de", cotangent, attn, preferred_element_type=jnp.float32)
    d_hidden = lax.optimization_barrier(
        jnp.einsum("vte,de->vtd", d_qkv, qkv_full, preferred_element_type=jnp.float32).astype(
            jnp.bfloat16
        )
    )
    grad_qkv, grad_out = (
        lax.psum_scatter(part_qkv, "tm", scatter_dimension=0, tiled=True),
        lax.psum_scatter(part_out, "tm", scatter_dimension=0, tiled=True),
    )
    mixed = (
        tok_float + jnp.einsum("vte,de->vtd", attn, out_full, preferred_element_type=jnp.float32)
    ).astype(jnp.bfloat16)
    grad = d_hidden.astype(jnp.float32) * norm_gain
    grad_tokens = cotangent.astype(jnp.float32) + inv_rms * (
        grad - normed * jnp.mean(grad * normed, -1, keepdims=True)
    )
    return (mixed, grad_tokens.astype(jnp.bfloat16), grad_qkv, grad_out)


def pid(x):
    return {"tm": x}


def place():
    me = lax.axis_index("tm")
    z, b = me // SPLIT, me % SPLIT
    return me, z, b, b // 2, b % 2


def greet(peers):
    barrier = pltpu.get_barrier_semaphore()
    for peer in peers:
        pl.semaphore_signal(barrier, inc=1, device_id=peer, device_id_type=MESH)
    pl.semaphore_wait(barrier, len(peers))


def remote(src, dst, send_sem, recv_sem, peer):
    return pltpu.make_async_remote_copy(
        src_ref=src,
        dst_ref=dst,
        send_sem=send_sem,
        recv_sem=recv_sem,
        device_id=peer,
        device_id_type=MESH,
    )


def gather_kernel(w_ref, out_ref, local_sem, send_z, send_y, send_x, send_c, recv):
    x = lax.axis_index("groups")
    me, z, b, y, c = place()
    over_z = [pid((z + dz) % FRAMES_HERE * SPLIT + b) for dz in range(1, FRAMES_HERE)]
    over_y = pid(z * SPLIT + (1 - y) * 2 + c)
    over_c = pid(z * SPLIT + y * 2 + (1 - c))
    over_x = {"groups": 1 - x}
    greet(over_z + [over_y, over_c, over_x])
    mine = (x, 2)
    started = []

    def send(src, t, k, sem, peer):
        copy = remote(src, out_ref.at[t, k], sem, recv.at[t, k], peer)
        copy.start()
        started.append(copy)

    def arrived(t, k, peer):
        remote(out_ref.at[t, k], out_ref.at[t, k], send_z.at[0, 0], recv.at[t, k], peer).wait_recv()

    local = [
        pltpu.make_async_copy(w_ref.at[t], out_ref.at[t, me], local_sem.at[i])
        for i, t in enumerate(mine)
    ]
    for copy in local:
        copy.start()
    for dz in range(1, FRAMES_HERE):
        for i, t in enumerate(mine):
            send(w_ref.at[t], t, me, send_z.at[i, dz], over_z[dz - 1])
    shards = [(z + FRAMES_HERE - dz) % FRAMES_HERE * SPLIT for dz in range(FRAMES_HERE)]
    order = [0, 1, 3, 2]
    for dz in order:
        k = shards[dz] + b
        for i, t in enumerate(mine):
            if dz:
                arrived(t, k, over_y)
            src = out_ref.at[t, k] if dz else w_ref.at[t]
            send(src, t, k, send_y.at[i, dz], over_y)
            if i == 0:
                send(src, t, k, send_x.at[0, dz], over_x)
            send(src, t, k, send_c.at[i, 0, dz], over_c)
    for dz in order:
        k = shards[dz] + (1 - y) * 2 + c
        for i, t in enumerate(mine):
            arrived(t, k, over_y)
            if i == 0:
                send(out_ref.at[t, k], t, k, send_x.at[1, dz], over_x)
            send(out_ref.at[t, k], t, k, send_c.at[i, 1, dz], over_c)
    for j in range(2):
        for dz in order:
            k = shards[dz] + (y if j == 0 else 1 - y) * 2 + c
            arrived(1 - x, k, over_x)
            send(out_ref.at[1 - x, k], 1 - x, k, send_c.at[2, j, dz], over_c)
    for t in range(3):
        for yy in range(2):
            for zz in range(FRAMES_HERE):
                arrived(t, zz * SPLIT + yy * 2 + (1 - c), over_c)
    for copy in local:
        copy.wait()
    for copy in started:
        copy.wait_send()


def gather_weights(blocks):
    owners = FRAMES_HERE * SPLIT
    dma = pltpu.SemaphoreType.DMA
    return pl.pallas_call(
        gather_kernel,
        out_shape=jax.ShapeDtypeStruct((3, owners) + blocks.shape[1:], blocks.dtype),
        in_specs=[pl.BlockSpec(memory_space=pl.ANY)],
        out_specs=pl.BlockSpec(memory_space=pl.ANY),
        scratch_shapes=[
            dma((2,)),
            dma((2, FRAMES_HERE)),
            dma((2, FRAMES_HERE)),
            dma((2, FRAMES_HERE)),
            dma((3, 2, FRAMES_HERE)),
            dma((3, owners)),
        ],
        compiler_params=pltpu.CompilerParams(collective_id=0, has_side_effects=True),
    )(blocks)


def forward_kernel(
    pay, keep, cols, pay_out, keep_out, cols_out, local_sem, send_z, recv_z, send_b, recv_b
):
    me, z, b, y, c = place()
    over_z = [pid((z + dz) % FRAMES_HERE * SPLIT + b) for dz in range(1, FRAMES_HERE)]
    over_b = [pid(z * SPLIT + (b + db) % SPLIT) for db in range(1, SPLIT)]
    greet(over_z + over_b)
    local = [
        pltpu.make_async_copy(pay.at[z], pay_out.at[z], local_sem.at[0]),
        pltpu.make_async_copy(keep.at[z], keep_out.at[z], local_sem.at[1]),
        pltpu.make_async_copy(cols.at[b], cols_out.at[b], local_sem.at[2]),
    ]
    copies = []
    for dz in (2, 1, 3):
        to = (z + dz) % FRAMES_HERE
        peer = over_z[dz - 1]
        copies.append(remote(keep.at[to], keep_out.at[z], send_z.at[1, dz], recv_z.at[1, dz], peer))
        copies.append(remote(pay.at[to], pay_out.at[z], send_z.at[0, dz], recv_z.at[0, dz], peer))
    for db in (2, 1, 3):
        to = (b + db) % SPLIT
        copies.append(
            remote(cols.at[to], cols_out.at[b], send_b.at[db], recv_b.at[db], over_b[db - 1])
        )
    for copy in copies + local:
        copy.start()
    for dz in (1, 2, 3):
        came = (z + FRAMES_HERE - dz) % FRAMES_HERE
        peer = over_z[dz - 1]
        remote(keep.at[z], keep_out.at[came], send_z.at[1, dz], recv_z.at[1, dz], peer).wait_recv()
        remote(pay.at[z], pay_out.at[came], send_z.at[0, dz], recv_z.at[0, dz], peer).wait_recv()
    for db in (1, 2, 3):
        came = (b + SPLIT - db) % SPLIT
        remote(cols.at[b], cols_out.at[came], send_b.at[db], recv_b.at[db], over_b[db - 1]).wait_recv()
    for copy in local:
        copy.wait()
    for copy in copies:
        copy.wait_send()


def send_forward(pay, keep, cols):
    dma = pltpu.SemaphoreType.DMA
    return pl.pallas_call(
        forward_kernel,
        out_shape=[jax.ShapeDtypeStruct(a.shape, a.dtype) for a in (pay, keep, cols)],
        in_specs=[pl.BlockSpec(memory_space=pl.ANY)] * 3,
        out_specs=[pl.BlockSpec(memory_space=pl.ANY)] * 3,
        scratch_shapes=[dma((3,)), dma((2, 4)), dma((2, 4)), dma((4,)), dma((4,))],
        compiler_params=pltpu.CompilerParams(collective_id=1, has_side_effects=True),
    )(pay, keep, cols)


def back_kernel(
    res, cols, own, sums, tok, left, part, came, extra,
    local_sem, send_z, send_y, send_c, recv, own_sem, send_p, recv_p, recv_x,
):
    f32, bf16 = jnp.float32, jnp.bfloat16
    me, z, b, y, c = place()
    over_z = [pid((z + dz) % FRAMES_HERE * SPLIT + b) for dz in range(1, FRAMES_HERE)]
    over_y = pid(z * SPLIT + (1 - y) * 2 + c)
    over_c = pid(z * SPLIT + y * 2 + (1 - c))
    greet(over_z + [over_y, over_c])
    block = BLOCK
    started = []
    width = res.shape[-1] // 4

    def lanes(t):
        return pl.ds(t * block, block)

    def send(src, t, i, j, sem, peer):
        slot = i * FRAMES_HERE + j
        copy = remote(src, tok.at[slot, :, lanes(t)], sem, recv.at[t, slot], peer)
        copy.start()
        started.append(copy)

    def arrived(t, i, j):
        slot = i * FRAMES_HERE + j
        place_at = tok.at[slot, :, lanes(t)]
        remote(place_at, place_at, send_z.at[0, 0], recv.at[t, slot], over_y).wait_recv()

    for t in range(3):
        for dz in (2, 1, 3):
            send(
                res.at[(z + dz) % FRAMES_HERE, :, lanes(t)],
                t, b, z, send_z.at[t, dz], over_z[dz - 1],
            )
    local = [
        pltpu.make_async_copy(res.at[z], tok.at[b * FRAMES_HERE + z], local_sem.at[0]),
        pltpu.make_async_copy(cols, left, local_sem.at[1]),
    ]
    for copy in local:
        copy.start()
    order = [0, 1, 3, 2]

    def from_z(t):
        for dz in order:
            j = (z + FRAMES_HERE - dz) % FRAMES_HERE
            if dz:
                arrived(t, b, j)
                src = tok.at[b * FRAMES_HERE + j, :, lanes(t)]
            else:
                src = res.at[z, :, lanes(t)]
            send(src, t, b, j, send_y.at[t, dz], over_y)
            send(src, t, b, j, send_c.at[t, 0, dz], over_c)

    def from_y(t):
        for dz in order:
            i, j = (1 - y) * 2 + c, (z + FRAMES_HERE - dz) % FRAMES_HERE
            arrived(t, i, j)
            src = tok.at[i * FRAMES_HERE + j, :, lanes(t)]
            send(src, t, i, j, send_c.at[t, 1, dz], over_c)

    def from_c(t):
        for yy in range(2):
            for j in range(FRAMES_HERE):
                arrived(t, yy * 2 + (1 - c), j)

    low = z < 2
    end = (z == 0) | (z == 3)

    def at(m):
        return jnp.where(low, m, 3 - m)

    def block_copy(t, owner, peer_z, to_extra):
        src = part.at[owner, :, lanes(t)]
        peer = pid(peer_z * SPLIT + b)
        if to_extra:
            return remote(src, extra.at[t], send_p.at[t, 2], recv_x.at[t], peer)
        return remote(src, came.at[t, z], send_p.at[t, 2], recv_p.at[t, z], peer)

    def near_copy(t, which):
        owner = jnp.where(end, at(1 + which), at(2 * which))
        src = part.at[owner, :, lanes(t)]
        peer = pid(owner * SPLIT + b)
        return remote(src, came.at[t, z], send_p.at[t, which], recv_p.at[t, z], peer)

    def contract(t):
        right = tok[:, :, lanes(t)].reshape(SPLIT, FRAMES_HERE * tok.shape[1], block)

        def over_tokens(kind):
            total = jnp.dot(left[0, kind], right[0], preferred_element_type=f32)
            for i in range(1, SPLIT):
                total += jnp.dot(left[i, kind], right[i], preferred_element_type=f32)
            return total

        product = over_tokens(0)
        if t == 0:
            lane = lax.broadcasted_iota(jnp.int32, product.shape, 1)
            product = jnp.where(lane < width, over_tokens(1), product)
        rows = part.shape[1]
        for owner in range(FRAMES_HERE):
            part[owner, :, t * block : (t + 1) * block] = product[owner * rows : (owner + 1) * rows]

        @pl.when(end)
        def _():
            block_copy(t, at(3), at(1), True).start()

        near_copy(t, 1).start()
        near_copy(t, 0).start()

    def pass_on(t):
        @pl.when(jnp.logical_not(end))
        def _():
            remote(extra.at[t], extra.at[t], send_p.at[t, 2], recv_x.at[t], over_y).wait_recv()
            far = at(3)
            part[far, :, t * block : (t + 1) * block] += extra[t]
            block_copy(t, far, far, False).start()

    from_z(0)
    from_y(0)
    from_z(1)
    for copy in local:
        copy.wait()
    from_c(0)
    contract(0)
    from_y(1)
    from_z(2)
    from_c(1)
    contract(1)
    pass_on(0)
    from_y(2)
    mine = pltpu.make_async_copy(tok.at[pl.ds(b * FRAMES_HERE, FRAMES_HERE)], own, own_sem)
    mine.start()
    from_c(2)
    contract(2)
    pass_on(1)
    pass_on(2)

    def landed(t, src):
        remote(
            came.at[t, src], came.at[t, src], send_p.at[t, 0], recv_p.at[t, src], over_y
        ).wait_recv()

    for t in range(3):
        here = slice(t * block, (t + 1) * block)

        @pl.when(end)
        def _():
            landed(t, at(1))
            landed(t, at(2))
            sums[:, here] = part[z, :, here] + came[t, at(1)] + came[t, at(2)]

        @pl.when(jnp.logical_not(end))
        def _():
            landed(t, at(0))
            landed(t, at(2))
            landed(t, at(3))
            sums[:, here] = (part[z, :, here] + came[t, at(0)]) + (came[t, at(2)] + came[t, at(3)])

    mine.wait()
    for copy in started:
        copy.wait_send()
    for t in range(3):
        near_copy(t, 0).wait_send()
        near_copy(t, 1).wait_send()

        @pl.when(end)
        def _():
            block_copy(t, at(3), at(1), True).wait_send()

        @pl.when(jnp.logical_not(end))
        def _():
            block_copy(t, at(3), at(3), False).wait_send()


def send_back(res, cols):
    dma = pltpu.SemaphoreType.DMA
    frames, rows, wide = res.shape
    shard = cols.shape[2] // frames
    f32 = jnp.float32
    flops = 2 * cols.shape[2] * SPLIT * cols.shape[3] * wide
    return pl.pallas_call(
        back_kernel,
        out_shape=[
            jax.ShapeDtypeStruct(res.shape, res.dtype),
            jax.ShapeDtypeStruct((shard, wide), f32),
        ],
        in_specs=[pl.BlockSpec(memory_space=pl.ANY)] * 2,
        out_specs=[
            pl.BlockSpec(memory_space=pl.ANY),
            pl.BlockSpec(memory_space=pltpu.VMEM),
        ],
        scratch_shapes=[
            pltpu.VMEM((SPLIT * frames, rows, wide), res.dtype),
            pltpu.VMEM(cols.shape, cols.dtype),
            pltpu.VMEM((frames, shard, wide), f32),
            pltpu.VMEM((3, frames, shard, wide // 3), f32),
            pltpu.VMEM((3, shard, wide // 3), f32),
            dma((2,)),
            dma((3, 4)),
            dma((3, 4)),
            dma((3, 2, 4)),
            dma((3, 16)),
            dma,
            dma((3, 3)),
            dma((3, 4)),
            dma((3,)),
        ],
        cost_estimate=pl.CostEstimate(flops=flops, bytes_accessed=4 * res.size, transcendentals=0),
        compiler_params=pltpu.CompilerParams(
            collective_id=2, has_side_effects=True, vmem_limit_bytes=40 * 1024 * 1024
        ),
    )(res, cols)


def attention_kernel(pay, allow, out, dk_sum, dv_sum):
    f32, bf16 = jnp.float32, jnp.bfloat16
    width = pay.shape[-1] // 4
    rows = pay.shape[1]
    scale = HD ** (-0.5)
    frames = pay.shape[0]
    row = lax.broadcasted_iota(jnp.int32, (width, 128), 0)
    lane = lax.broadcasted_iota(jnp.int32, (width, 128), 1)
    gather = ((row >= lane * HD) & (row < lane * HD + HD)).astype(f32).astype(bf16)
    row_t = lax.broadcasted_iota(jnp.int32, (128, width), 1)
    lane_t = lax.broadcasted_iota(jnp.int32, (128, width), 0)
    spread = ((row_t >= lane_t * HD) & (row_t < lane_t * HD + HD)).astype(f32).astype(bf16)

    def part(i, f):
        return pay[f, :, i * width : (i + 1) * width].astype(f32)

    def head_sums(prod):
        high = prod.astype(bf16)
        low = (prod - high.astype(f32)).astype(bf16)
        return jnp.dot(high, gather, preferred_element_type=f32) + jnp.dot(
            low, gather, preferred_element_type=f32
        )

    for f in range(frames):
        query, d_out = part(1, f), part(0, f)
        scores, dprob = [], []
        for g in range(frames):
            raw = head_sums(query * part(2, g)) * scale
            scores.append(jnp.where(allow[f * frames + g] > 0, raw, -1e30))
            dprob.append(head_sums(d_out * part(3, g)))
        top = functools.reduce(jnp.maximum, scores)
        expo = [jnp.exp(s - top) for s in scores]
        total = functools.reduce(jnp.add, expo)
        probs = [e / total for e in expo]
        inner = functools.reduce(jnp.add, [p * d for p, d in zip(probs, dprob)])
        attn = jnp.zeros((rows, width), f32)
        d_query = jnp.zeros((rows, width), f32)
        for g in range(frames):
            pb = jnp.dot(probs[g].astype(bf16), spread, preferred_element_type=f32)
            dscore = (probs[g] * (dprob[g] - inner)).astype(bf16)
            ds = jnp.dot(dscore, spread, preferred_element_type=f32)
            attn += pb * part(3, g)
            d_query += ds * part(2, g)
            if f == 0:
                dk_sum[g] = ds * query
                dv_sum[g] = pb * d_out
            else:
                dk_sum[g] += ds * query
                dv_sum[g] += pb * d_out
        out[f, :, 0:width] = attn.astype(bf16)
        out[f, :, width : 2 * width] = (d_query * scale).astype(bf16)
    for g in range(frames):
        out[g, :, 2 * width : 3 * width] = (dk_sum[g] * scale).astype(bf16)
        out[g, :, 3 * width : 4 * width] = dv_sum[g].astype(bf16)


def attention(pay, allow):
    frames, rows, wide = pay.shape
    return pl.pallas_call(
        attention_kernel,
        out_shape=jax.ShapeDtypeStruct(pay.shape, pay.dtype),
        in_specs=[pl.BlockSpec(memory_space=pltpu.VMEM)] * 2,
        out_specs=pl.BlockSpec(memory_space=pltpu.VMEM),
        scratch_shapes=[pltpu.VMEM((frames, rows, wide // 4), jnp.float32)] * 2,
        compiler_params=pltpu.CompilerParams(vmem_limit_bytes=32 * 1024 * 1024),
    )(pay, allow)


def four_frames(tokens, norm_gain, w_qkv, w_out, block_mask, keep_tiles, cotangent):
    f32, bf16 = jnp.float32, jnp.bfloat16
    frames = FRAMES_HERE
    tokens, cotangent = tokens[0], cotangent[0]
    band, model = tokens.shape
    shard, wide_qkv = w_qkv.shape
    wide = wide_qkv + w_out.shape[1]
    rows = band // frames
    width = wide // 4
    blocks = jnp.concatenate([w_out, w_qkv], 1).reshape(shard, 3, BLOCK).transpose(1, 0, 2)
    gathered = gather_weights(blocks)
    weights = [gathered[t].reshape(model, BLOCK) for t in range(3)]

    tok_float = tokens.astype(f32)
    inv_rms = lax.rsqrt(jnp.mean(tok_float * tok_float, -1, keepdims=True) + EPS)
    normed = tok_float * inv_rms
    hidden = (normed * norm_gain).astype(bf16)
    is_attn = jnp.arange(BLOCK) < width

    def project(a, t):
        return jnp.dot(a, weights[t], preferred_element_type=f32)

    first = jnp.where(is_attn, project(cotangent, 0), project(hidden, 0))
    pay = jnp.concatenate(
        [first.astype(bf16), project(hidden, 1).astype(bf16), project(hidden, 2).astype(bf16)], 1
    ).reshape(frames, rows, wide)
    keep = jnp.repeat(keep_tiles[0].astype(f32), TILE).reshape(frames, 1, rows)
    keep = jnp.pad(jnp.broadcast_to(keep, (frames, 8, rows)), ((0, 0), (0, 0), (0, 128 - rows)))

    def owners_columns(a):
        cut = a.T.reshape(frames, SPLIT, shard, band)
        return cut.transpose(1, 0, 2, 3).reshape(SPLIT, 1, frames * shard, band)

    cols = jnp.concatenate([owners_columns(hidden), owners_columns(cotangent)], 1)
    pay_at, keep_at, cols_at = send_forward(pay, keep, cols)

    frame_block = jnp.arange(frames) // TB
    same_block = frame_block[:, None] == frame_block[None, :]
    seen = (jnp.repeat(jnp.repeat(block_mask[0], TB, 0), TB, 1) > 0) | same_block
    diag_one = jnp.arange(frames)[:, None] == jnp.arange(frames)[None, :]
    kept = keep_at[:, 0, :rows] > 0
    allow = seen[:, :, None] & (kept[None] | diag_one[:, :, None])
    allow = jnp.broadcast_to(
        allow.reshape(frames * frames, rows, 1).astype(f32), (frames * frames, rows, 128)
    )
    own, sums = send_back(attention(pay_at, allow), cols_at)
    grad_out, grad_qkv = sums[:, :width], sums[:, width:]
    own = own.reshape(band, wide)
    results = [own[:, t * BLOCK : (t + 1) * BLOCK] for t in range(3)]
    zero = jnp.zeros((), bf16)

    def project_back(a, t):
        return lax.dot_general(a, weights[t], (((1,), (1,)), ((), ())), preferred_element_type=f32)

    d_hidden = lax.optimization_barrier(
        (
            project_back(jnp.where(is_attn, zero, results[0]), 0)
            + project_back(results[1], 1)
            + project_back(results[2], 2)
        ).astype(bf16)
    )
    mixed = (tok_float + project_back(jnp.where(is_attn, results[0], zero), 0)).astype(bf16)
    grad = d_hidden.astype(f32) * norm_gain
    grad_tokens = cotangent.astype(f32) + inv_rms * (
        grad - normed * jnp.mean(grad * normed, -1, keepdims=True)
    )
    return (mixed[None], grad_tokens.astype(bf16)[None], grad_qkv, grad_out)


def solution(mesh):
    placed = (
        P("groups", "tm", None),
        P(),
        P("tm", None),
        P("tm", None),
        P("groups", None, None),
        P("groups", "tm"),
        P("groups", "tm", None),
    )
    small = mesh.shape["tm"] == FRAMES_HERE * SPLIT and mesh.shape["groups"] == 2
    return jax.shard_map(
        four_frames if small else per_device,
        mesh=mesh,
        in_specs=placed,
        out_specs=(
            P("groups", "tm", None),
            P("groups", "tm", None),
            P(("groups", "tm"), None),
            P(("groups", "tm"), None),
        ),
        check_vma=False,
    )
```

```python
import functools

import jax
import jax.numpy as jnp
from jax import lax
from jax.experimental import pallas as pl
from jax.experimental.pallas import tpu as pltpu
from jax.sharding import PartitionSpec as P

HD = 72
SPLIT = 4
TB = 2
TILE = 16


EPS = 1e-06
FRAMES_HERE = 4
BLOCK = 768
MESH = pl.DeviceIdType.MESH


def temporal(qkv_cols, dattn_cols, keep_cols, block_mask, frames):
    videos, per_owner, owners, _ = qkv_cols.shape
    band_count = owners // frames
    heads_n = dattn_cols.shape[-1] // HD
    scale = HD ** (-0.5)
    parts = qkv_cols.reshape(videos, per_owner, frames, band_count, 3, heads_n, HD)
    queries = parts[:, :, :, :, 0]
    key_part = parts[:, :, :, :, 1]
    val_part = parts[:, :, :, :, 2]
    d_out = dattn_cols.reshape(videos, per_owner, frames, band_count, heads_n, HD)
    frame_block = jnp.arange(frames) // TB
    blocks = jnp.repeat(jnp.repeat(block_mask, TB, 1), TB, 2) > 0
    same_block = frame_block[:, None] == frame_block[None, :]
    block_allow = blocks | same_block[None]
    kept = jnp.transpose(keep_cols.reshape(videos, per_owner, frames, band_count) > 0, (0, 1, 3, 2))
    diag_one = jnp.arange(frames)[:, None] == jnp.arange(frames)[None, :]
    allow = block_allow[:, None, None, None, :, :] & (kept[:, :, :, None, None, :] | diag_one)
    scores = (
        jnp.einsum("vrfshd,vrgshd->vrshfg", queries, key_part, preferred_element_type=jnp.float32)
        * scale
    )
    scores = jnp.where(allow, scores, -1e30)
    row_top = jnp.max(scores, -1, keepdims=True)
    expo = jnp.exp(scores - row_top)
    probs = expo / jnp.sum(expo, -1, keepdims=True)
    probs_b = probs.astype(jnp.bfloat16)
    attn = jnp.einsum(
        "vrshfg,vrgshd->vrfshd", probs_b, val_part, preferred_element_type=jnp.float32
    ).astype(jnp.bfloat16)
    dprob = jnp.einsum("vrfshd,vrgshd->vrshfg", d_out, val_part, preferred_element_type=jnp.float32)
    dscore = probs * (dprob - jnp.sum(probs * dprob, -1, keepdims=True))
    dscore_b = dscore.astype(jnp.bfloat16)
    grad_query = (
        jnp.einsum("vrshfg,vrgshd->vrfshd", dscore_b, key_part, preferred_element_type=jnp.float32)
        * scale
    ).astype(jnp.bfloat16)
    grad_key = (
        jnp.einsum("vrshfg,vrfshd->vrgshd", dscore_b, queries, preferred_element_type=jnp.float32)
        * scale
    ).astype(jnp.bfloat16)
    grad_value = jnp.einsum(
        "vrshfg,vrfshd->vrgshd", probs_b, d_out, preferred_element_type=jnp.float32
    ).astype(jnp.bfloat16)
    d_qkv = jnp.stack([grad_query, grad_key, grad_value], axis=4).reshape(
        videos, per_owner, owners, -1
    )
    return (attn.reshape(videos, per_owner, owners, -1), d_qkv)


def per_device(tokens, norm_gain, w_qkv, w_out, block_mask, keep_tiles, cotangent):
    owners = lax.axis_size("tm")
    videos, band_len, model_width = tokens.shape
    per_owner = band_len // owners
    frames = owners // SPLIT
    qkv_full, out_full = (
        lax.all_gather(w_qkv, "tm", axis=0, tiled=True),
        lax.all_gather(w_out, "tm", axis=0, tiled=True),
    )
    tok_float = tokens.astype(jnp.float32)
    inv_rms = lax.rsqrt(jnp.mean(tok_float * tok_float, -1, keepdims=True) + EPS)
    normed = tok_float * inv_rms
    hidden = (normed * norm_gain).astype(jnp.bfloat16)
    keep_tok = jnp.repeat(keep_tiles, TILE, axis=1).reshape(videos, per_owner, owners)
    qkv = jnp.dot(hidden, qkv_full, preferred_element_type=jnp.float32).astype(jnp.bfloat16)
    d_attn = jnp.dot(cotangent, out_full, preferred_element_type=jnp.float32).astype(jnp.bfloat16)
    qkv_cols, dattn_cols, keep_cols = (
        lax.all_to_all(
            qkv.reshape(videos, per_owner, owners, -1),
            "tm",
            split_axis=2,
            concat_axis=2,
            tiled=True,
        ),
        lax.all_to_all(
            d_attn.reshape(videos, per_owner, owners, -1),
            "tm",
            split_axis=2,
            concat_axis=2,
            tiled=True,
        ),
        lax.all_to_all(keep_tok, "tm", split_axis=2, concat_axis=2, tiled=True),
    )
    attn_cols, dqkv_cols = temporal(qkv_cols, dattn_cols, keep_cols, block_mask, frames)
    attn_rows, dqkv_rows = (
        lax.all_to_all(attn_cols, "tm", split_axis=2, concat_axis=2, tiled=True),
        lax.all_to_all(dqkv_cols, "tm", split_axis=2, concat_axis=2, tiled=True),
    )
    attn = attn_rows.reshape(videos, band_len, -1)
    d_qkv = dqkv_rows.reshape(videos, band_len, -1)
    part_qkv = jnp.einsum("vtd,vte->de", hidden, d_qkv, preferred_element_type=jnp.float32)
    part_out = jnp.einsum("vtd,vte->de", cotangent, attn, preferred_element_type=jnp.float32)
    d_hidden = lax.optimization_barrier(
        jnp.einsum("vte,de->vtd", d_qkv, qkv_full, preferred_element_type=jnp.float32).astype(
            jnp.bfloat16
        )
    )
    grad_qkv, grad_out = (
        lax.psum_scatter(part_qkv, "tm", scatter_dimension=0, tiled=True),
        lax.psum_scatter(part_out, "tm", scatter_dimension=0, tiled=True),
    )
    mixed = (
        tok_float + jnp.einsum("vte,de->vtd", attn, out_full, preferred_element_type=jnp.float32)
    ).astype(jnp.bfloat16)
    grad = d_hidden.astype(jnp.float32) * norm_gain
    grad_tokens = cotangent.astype(jnp.float32) + inv_rms * (
        grad - normed * jnp.mean(grad * normed, -1, keepdims=True)
    )
    return (mixed, grad_tokens.astype(jnp.bfloat16), grad_qkv, grad_out)


def pid(x):
    return {"tm": x}


def place():
    me = lax.axis_index("tm")
    z, b = me // SPLIT, me % SPLIT
    return me, z, b, b // 2, b % 2


def greet(peers):
    barrier = pltpu.get_barrier_semaphore()
    for peer in peers:
        pl.semaphore_signal(barrier, inc=1, device_id=peer, device_id_type=MESH)
    pl.semaphore_wait(barrier, len(peers))


def remote(src, dst, send_sem, recv_sem, peer):
    return pltpu.make_async_remote_copy(
        src_ref=src,
        dst_ref=dst,
        send_sem=send_sem,
        recv_sem=recv_sem,
        device_id=peer,
        device_id_type=MESH,
    )


def forward_kernel(
    w_ref, cols, keep, w_out, pay_out, keep_out, cols_out, held, left, pay,
    local_sem, send_z, send_y, send_x, send_c, recv, save_sem,
    send_k, recv_k, send_b, recv_b, send_p, recv_p, own_sem,
):
    f32 = jnp.float32
    x = lax.axis_index("groups")
    me, z, b, y, c = place()
    over_z = [pid((z + dz) % FRAMES_HERE * SPLIT + b) for dz in range(1, FRAMES_HERE)]
    over_b = [pid(z * SPLIT + (b + db) % SPLIT) for db in range(1, SPLIT)]
    over_y = pid(z * SPLIT + (1 - y) * 2 + c)
    over_c = pid(z * SPLIT + y * 2 + (1 - c))
    over_x = {"groups": 1 - x}
    greet(over_z + over_b + [over_x])
    blocks = (2, x, 1 - x)
    started = []

    def start(copy):
        copy.start()
        started.append(copy)

    def send(src, t, k, sem, peer):
        start(remote(src, held.at[t, k], sem, recv.at[t, k], peer))

    def arrived(t, k):
        remote(held.at[t, k], held.at[t, k], send_z.at[0, 0], recv.at[t, k], over_y).wait_recv()

    local = [
        pltpu.make_async_copy(w_ref.at[2], held.at[2, me], local_sem.at[0]),
        pltpu.make_async_copy(w_ref.at[x], held.at[x, me], local_sem.at[1]),
        pltpu.make_async_copy(cols, left, local_sem.at[2]),
        pltpu.make_async_copy(keep.at[z], keep_out.at[z], local_sem.at[3]),
        pltpu.make_async_copy(cols.at[b], cols_out.at[b], local_sem.at[4]),
    ]
    for copy in local:
        copy.start()
    for i in range(2):
        for dz in (2, 1, 3):
            send(w_ref.at[blocks[i]], blocks[i], me, send_z.at[i, dz], over_z[dz - 1])
    shards = [(z + FRAMES_HERE - dz) % FRAMES_HERE * SPLIT for dz in range(FRAMES_HERE)]
    order = [0, 1, 3, 2]

    def from_z(i):
        t = blocks[i]
        for dz in order:
            k = shards[dz] + b
            if dz:
                arrived(t, k)
            src = held.at[t, k] if dz else w_ref.at[t]
            send(src, t, k, send_y.at[i, dz], over_y)
            if i == 1:
                send(src, t, k, send_x.at[0, dz], over_x)
            send(src, t, k, send_c.at[i, 0, dz], over_c)

    def from_y(i):
        t = blocks[i]
        for dz in order:
            k = shards[dz] + (1 - y) * 2 + c
            arrived(t, k)
            if i == 1:
                send(held.at[t, k], t, k, send_x.at[1, dz], over_x)
            send(held.at[t, k], t, k, send_c.at[i, 1, dz], over_c)

    def from_x(j):
        t = blocks[2]
        for dz in order:
            k = shards[dz] + (y if j == 0 else 1 - y) * 2 + c
            arrived(t, k)
            send(held.at[t, k], t, k, send_c.at[2, j, dz], over_c)

    rows = pay.shape[2]
    width = 3 * BLOCK // 4
    own = []

    def project(i):
        t = blocks[i]
        for yy in range(2):
            for zz in range(FRAMES_HERE):
                arrived(t, zz * SPLIT + yy * 2 + (1 - c))
        save = pltpu.make_async_copy(held.at[t], w_out.at[t], save_sem.at[i])
        save.start()
        own.append(save)

        def over_shards(kind):
            total = None
            for k in range(FRAMES_HERE * SPLIT):
                term = lax.dot_general(
                    left[k % SPLIT, kind, k // SPLIT],
                    held[t, k],
                    (((0,), (0,)), ((), ())),
                    preferred_element_type=f32,
                )
                total = term if total is None else total + term
            return total

        def store(value):
            value = value.astype(pay.dtype)
            for to in range(FRAMES_HERE):
                pay[t, to] = value[to * rows : (to + 1) * rows]

        if i == 0:
            store(over_shards(0))
        else:

            @pl.when(t != 0)
            def _():
                store(over_shards(0))

            @pl.when(t == 0)
            def _():
                value = over_shards(0)
                lane = lax.broadcasted_iota(jnp.int32, value.shape, 1)
                store(jnp.where(lane < width, over_shards(1), value))

        lanes = pl.ds(pl.multiple_of(t * BLOCK, BLOCK), BLOCK)
        for dz in (2, 1, 3):
            start(
                remote(
                    pay.at[t, (z + dz) % FRAMES_HERE],
                    pay_out.at[z, :, lanes],
                    send_p.at[i, dz],
                    recv_p.at[i, dz],
                    over_z[dz - 1],
                )
            )
        keep_own = pltpu.make_async_copy(pay.at[t, z], pay_out.at[z, :, lanes], own_sem.at[i])
        keep_own.start()
        own.append(keep_own)

    from_z(0)
    from_y(0)
    from_z(1)
    for copy in local:
        copy.wait()
    project(0)
    from_y(1)
    from_x(0)
    for dz in (2, 1, 3):
        to = (z + dz) % FRAMES_HERE
        start(
            remote(keep.at[to], keep_out.at[z], send_k.at[dz], recv_k.at[dz], over_z[dz - 1])
        )
    for db in (2, 1, 3):
        to = (b + db) % SPLIT
        start(remote(cols.at[to], cols_out.at[b], send_b.at[db], recv_b.at[db], over_b[db - 1]))
    project(1)
    from_x(1)
    project(2)
    for dz in (1, 2, 3):
        came = (z + FRAMES_HERE - dz) % FRAMES_HERE
        peer = over_z[dz - 1]
        remote(keep.at[z], keep_out.at[came], send_k.at[dz], recv_k.at[dz], peer).wait_recv()
        for i in range(3):
            lanes = pl.ds(pl.multiple_of(blocks[i] * BLOCK, BLOCK), BLOCK)
            remote(
                pay.at[blocks[i], z],
                pay_out.at[came, :, lanes],
                send_p.at[i, dz],
                recv_p.at[i, dz],
                peer,
            ).wait_recv()
    for db in (1, 2, 3):
        came = (b + SPLIT - db) % SPLIT
        remote(cols.at[b], cols_out.at[came], send_b.at[db], recv_b.at[db], over_b[db - 1]).wait_recv()
    for copy in own:
        copy.wait()
    for copy in started:
        copy.wait_send()


def forward(blocks, cols, keep):
    owners = FRAMES_HERE * SPLIT
    dma = pltpu.SemaphoreType.DMA
    shard = blocks.shape[1]
    rows = cols.shape[-1] // FRAMES_HERE
    held = (3, owners, shard, BLOCK)
    pay = (FRAMES_HERE, rows, 3 * BLOCK)
    return pl.pallas_call(
        forward_kernel,
        out_shape=[
            jax.ShapeDtypeStruct(held, blocks.dtype),
            jax.ShapeDtypeStruct(pay, blocks.dtype),
            jax.ShapeDtypeStruct(keep.shape, keep.dtype),
            jax.ShapeDtypeStruct(cols.shape, cols.dtype),
        ],
        in_specs=[pl.BlockSpec(memory_space=pl.ANY)] * 3,
        out_specs=[pl.BlockSpec(memory_space=pl.ANY)] * 4,
        scratch_shapes=[
            pltpu.VMEM(held, blocks.dtype),
            pltpu.VMEM(cols.shape, cols.dtype),
            pltpu.VMEM((3, FRAMES_HERE, rows, BLOCK), blocks.dtype),
            dma((5,)),
            dma((2, 4)),
            dma((2, 4)),
            dma((2, 4)),
            dma((3, 2, 4)),
            dma((3, owners)),
            dma((3,)),
            dma((4,)),
            dma((4,)),
            dma((4,)),
            dma((4,)),
            dma((3, 4)),
            dma((3, 4)),
            dma((3,)),
        ],
        compiler_params=pltpu.CompilerParams(
            collective_id=0, has_side_effects=True, vmem_limit_bytes=40 * 1024 * 1024
        ),
    )(blocks, cols, keep)


def back_kernel(
    res, cols, own, sums, tok, left, part, came, extra,
    local_sem, send_z, send_y, send_c, recv, own_sem, send_p, recv_p, recv_x,
):
    f32, bf16 = jnp.float32, jnp.bfloat16
    me, z, b, y, c = place()
    over_z = [pid((z + dz) % FRAMES_HERE * SPLIT + b) for dz in range(1, FRAMES_HERE)]
    over_y = pid(z * SPLIT + (1 - y) * 2 + c)
    over_c = pid(z * SPLIT + y * 2 + (1 - c))
    greet(over_z + [over_y, over_c])
    block = BLOCK
    started = []
    width = res.shape[-1] // 4

    def lanes(t):
        return pl.ds(t * block, block)

    def send(src, t, i, j, sem, peer):
        slot = i * FRAMES_HERE + j
        copy = remote(src, tok.at[slot, :, lanes(t)], sem, recv.at[t, slot], peer)
        copy.start()
        started.append(copy)

    def arrived(t, i, j):
        slot = i * FRAMES_HERE + j
        place_at = tok.at[slot, :, lanes(t)]
        remote(place_at, place_at, send_z.at[0, 0], recv.at[t, slot], over_y).wait_recv()

    for t in range(3):
        for dz in (2, 1, 3):
            send(
                res.at[(z + dz) % FRAMES_HERE, :, lanes(t)],
                t, b, z, send_z.at[t, dz], over_z[dz - 1],
            )
    local = [
        pltpu.make_async_copy(res.at[z], tok.at[b * FRAMES_HERE + z], local_sem.at[0]),
        pltpu.make_async_copy(cols, left, local_sem.at[1]),
    ]
    for copy in local:
        copy.start()
    order = [0, 1, 3, 2]

    def from_z(t):
        for dz in order:
            j = (z + FRAMES_HERE - dz) % FRAMES_HERE
            if dz:
                arrived(t, b, j)
                src = tok.at[b * FRAMES_HERE + j, :, lanes(t)]
            else:
                src = res.at[z, :, lanes(t)]
            send(src, t, b, j, send_y.at[t, dz], over_y)
            send(src, t, b, j, send_c.at[t, 0, dz], over_c)

    def from_y(t):
        for dz in order:
            i, j = (1 - y) * 2 + c, (z + FRAMES_HERE - dz) % FRAMES_HERE
            arrived(t, i, j)
            src = tok.at[i * FRAMES_HERE + j, :, lanes(t)]
            send(src, t, i, j, send_c.at[t, 1, dz], over_c)

    def from_c(t):
        for yy in range(2):
            for j in range(FRAMES_HERE):
                arrived(t, yy * 2 + (1 - c), j)

    low = z < 2
    end = (z == 0) | (z == 3)

    def at(m):
        return jnp.where(low, m, 3 - m)

    def block_copy(t, owner, peer_z, to_extra):
        src = part.at[owner, :, lanes(t)]
        peer = pid(peer_z * SPLIT + b)
        if to_extra:
            return remote(src, extra.at[t], send_p.at[t, 2], recv_x.at[t], peer)
        return remote(src, came.at[t, z], send_p.at[t, 2], recv_p.at[t, z], peer)

    def near_copy(t, which):
        owner = jnp.where(end, at(1 + which), at(2 * which))
        src = part.at[owner, :, lanes(t)]
        peer = pid(owner * SPLIT + b)
        return remote(src, came.at[t, z], send_p.at[t, which], recv_p.at[t, z], peer)

    def contract(t):
        right = tok[:, :, lanes(t)].reshape(SPLIT, FRAMES_HERE * tok.shape[1], block)

        def over_tokens(kind):
            total = jnp.dot(left[0, kind], right[0], preferred_element_type=f32)
            for i in range(1, SPLIT):
                total += jnp.dot(left[i, kind], right[i], preferred_element_type=f32)
            return total

        product = over_tokens(0)
        if t == 0:
            lane = lax.broadcasted_iota(jnp.int32, product.shape, 1)
            product = jnp.where(lane < width, over_tokens(1), product)
        rows = part.shape[1]
        for owner in range(FRAMES_HERE):
            part[owner, :, t * block : (t + 1) * block] = product[owner * rows : (owner + 1) * rows]

        @pl.when(end)
        def _():
            block_copy(t, at(3), at(1), True).start()

        near_copy(t, 1).start()
        near_copy(t, 0).start()

    def pass_on(t):
        @pl.when(jnp.logical_not(end))
        def _():
            remote(extra.at[t], extra.at[t], send_p.at[t, 2], recv_x.at[t], over_y).wait_recv()
            far = at(3)
            part[far, :, t * block : (t + 1) * block] += extra[t]
            block_copy(t, far, far, False).start()

    from_z(0)
    from_y(0)
    from_z(1)
    for copy in local:
        copy.wait()
    from_c(0)
    contract(0)
    from_y(1)
    from_z(2)
    from_c(1)
    contract(1)
    pass_on(0)
    from_y(2)
    mine = pltpu.make_async_copy(tok.at[pl.ds(b * FRAMES_HERE, FRAMES_HERE)], own, own_sem)
    mine.start()
    from_c(2)
    contract(2)
    pass_on(1)
    pass_on(2)

    def landed(t, src):
        remote(
            came.at[t, src], came.at[t, src], send_p.at[t, 0], recv_p.at[t, src], over_y
        ).wait_recv()

    for t in range(3):
        here = slice(t * block, (t + 1) * block)

        @pl.when(end)
        def _():
            landed(t, at(1))
            landed(t, at(2))
            sums[:, here] = part[z, :, here] + came[t, at(1)] + came[t, at(2)]

        @pl.when(jnp.logical_not(end))
        def _():
            landed(t, at(0))
            landed(t, at(2))
            landed(t, at(3))
            sums[:, here] = (part[z, :, here] + came[t, at(0)]) + (came[t, at(2)] + came[t, at(3)])

    mine.wait()
    for copy in started:
        copy.wait_send()
    for t in range(3):
        near_copy(t, 0).wait_send()
        near_copy(t, 1).wait_send()

        @pl.when(end)
        def _():
            block_copy(t, at(3), at(1), True).wait_send()

        @pl.when(jnp.logical_not(end))
        def _():
            block_copy(t, at(3), at(3), False).wait_send()


def send_back(res, cols):
    dma = pltpu.SemaphoreType.DMA
    frames, rows, wide = res.shape
    shard = cols.shape[2] // frames
    f32 = jnp.float32
    flops = 2 * cols.shape[2] * SPLIT * cols.shape[3] * wide
    return pl.pallas_call(
        back_kernel,
        out_shape=[
            jax.ShapeDtypeStruct(res.shape, res.dtype),
            jax.ShapeDtypeStruct((shard, wide), f32),
        ],
        in_specs=[pl.BlockSpec(memory_space=pl.ANY)] * 2,
        out_specs=[
            pl.BlockSpec(memory_space=pl.ANY),
            pl.BlockSpec(memory_space=pltpu.VMEM),
        ],
        scratch_shapes=[
            pltpu.VMEM((SPLIT * frames, rows, wide), res.dtype),
            pltpu.VMEM(cols.shape, cols.dtype),
            pltpu.VMEM((frames, shard, wide), f32),
            pltpu.VMEM((3, frames, shard, wide // 3), f32),
            pltpu.VMEM((3, shard, wide // 3), f32),
            dma((2,)),
            dma((3, 4)),
            dma((3, 4)),
            dma((3, 2, 4)),
            dma((3, 16)),
            dma,
            dma((3, 3)),
            dma((3, 4)),
            dma((3,)),
        ],
        cost_estimate=pl.CostEstimate(flops=flops, bytes_accessed=4 * res.size, transcendentals=0),
        compiler_params=pltpu.CompilerParams(
            collective_id=2, has_side_effects=True, vmem_limit_bytes=40 * 1024 * 1024
        ),
    )(res, cols)


def attention_kernel(pay, allow, out, dk_sum, dv_sum):
    f32, bf16 = jnp.float32, jnp.bfloat16
    width = pay.shape[-1] // 4
    rows = pay.shape[1]
    scale = HD ** (-0.5)
    frames = pay.shape[0]
    row = lax.broadcasted_iota(jnp.int32, (width, 128), 0)
    lane = lax.broadcasted_iota(jnp.int32, (width, 128), 1)
    gather = ((row >= lane * HD) & (row < lane * HD + HD)).astype(f32).astype(bf16)
    row_t = lax.broadcasted_iota(jnp.int32, (128, width), 1)
    lane_t = lax.broadcasted_iota(jnp.int32, (128, width), 0)
    spread = ((row_t >= lane_t * HD) & (row_t < lane_t * HD + HD)).astype(f32).astype(bf16)

    def part(i, f):
        return pay[f, :, i * width : (i + 1) * width].astype(f32)

    def head_sums(prod):
        high = prod.astype(bf16)
        low = (prod - high.astype(f32)).astype(bf16)
        return jnp.dot(high, gather, preferred_element_type=f32) + jnp.dot(
            low, gather, preferred_element_type=f32
        )

    for f in range(frames):
        query, d_out = part(1, f), part(0, f)
        scores, dprob = [], []
        for g in range(frames):
            raw = head_sums(query * part(2, g)) * scale
            scores.append(jnp.where(allow[f * frames + g] > 0, raw, -1e30))
            dprob.append(head_sums(d_out * part(3, g)))
        top = functools.reduce(jnp.maximum, scores)
        expo = [jnp.exp(s - top) for s in scores]
        total = functools.reduce(jnp.add, expo)
        probs = [e / total for e in expo]
        inner = functools.reduce(jnp.add, [p * d for p, d in zip(probs, dprob)])
        attn = jnp.zeros((rows, width), f32)
        d_query = jnp.zeros((rows, width), f32)
        for g in range(frames):
            pb = jnp.dot(probs[g].astype(bf16), spread, preferred_element_type=f32)
            dscore = (probs[g] * (dprob[g] - inner)).astype(bf16)
            ds = jnp.dot(dscore, spread, preferred_element_type=f32)
            attn += pb * part(3, g)
            d_query += ds * part(2, g)
            if f == 0:
                dk_sum[g] = ds * query
                dv_sum[g] = pb * d_out
            else:
                dk_sum[g] += ds * query
                dv_sum[g] += pb * d_out
        out[f, :, 0:width] = attn.astype(bf16)
        out[f, :, width : 2 * width] = (d_query * scale).astype(bf16)
    for g in range(frames):
        out[g, :, 2 * width : 3 * width] = (dk_sum[g] * scale).astype(bf16)
        out[g, :, 3 * width : 4 * width] = dv_sum[g].astype(bf16)


def attention(pay, allow):
    frames, rows, wide = pay.shape
    return pl.pallas_call(
        attention_kernel,
        out_shape=jax.ShapeDtypeStruct(pay.shape, pay.dtype),
        in_specs=[pl.BlockSpec(memory_space=pltpu.VMEM)] * 2,
        out_specs=pl.BlockSpec(memory_space=pltpu.VMEM),
        scratch_shapes=[pltpu.VMEM((frames, rows, wide // 4), jnp.float32)] * 2,
        compiler_params=pltpu.CompilerParams(vmem_limit_bytes=32 * 1024 * 1024),
    )(pay, allow)


def four_frames(tokens, norm_gain, w_qkv, w_out, block_mask, keep_tiles, cotangent):
    f32, bf16 = jnp.float32, jnp.bfloat16
    frames = FRAMES_HERE
    tokens, cotangent = tokens[0], cotangent[0]
    band, model = tokens.shape
    shard, wide_qkv = w_qkv.shape
    wide = wide_qkv + w_out.shape[1]
    rows = band // frames
    width = wide // 4
    blocks = jnp.concatenate([w_out, w_qkv], 1).reshape(shard, 3, BLOCK).transpose(1, 0, 2)
    tok_float = tokens.astype(f32)
    inv_rms = lax.rsqrt(jnp.mean(tok_float * tok_float, -1, keepdims=True) + EPS)
    normed = tok_float * inv_rms
    hidden = (normed * norm_gain).astype(bf16)
    is_attn = jnp.arange(BLOCK) < width
    keep = jnp.repeat(keep_tiles[0].astype(f32), TILE).reshape(frames, 1, rows)
    keep = jnp.pad(jnp.broadcast_to(keep, (frames, 8, rows)), ((0, 0), (0, 0), (0, 128 - rows)))

    def owners_columns(a):
        cut = a.T.reshape(frames, SPLIT, shard, band)
        return cut.transpose(1, 0, 2, 3)[:, None]

    cols = jnp.concatenate([owners_columns(hidden), owners_columns(cotangent)], 1)
    gathered, pay_at, keep_at, cols_at = forward(blocks, cols, keep)
    weights = [gathered[t].reshape(model, BLOCK) for t in range(3)]
    cols_at = cols_at.reshape(SPLIT, 2, frames * shard, band)

    frame_block = jnp.arange(frames) // TB
    same_block = frame_block[:, None] == frame_block[None, :]
    seen = (jnp.repeat(jnp.repeat(block_mask[0], TB, 0), TB, 1) > 0) | same_block
    diag_one = jnp.arange(frames)[:, None] == jnp.arange(frames)[None, :]
    kept = keep_at[:, 0, :rows] > 0
    allow = seen[:, :, None] & (kept[None] | diag_one[:, :, None])
    allow = jnp.broadcast_to(
        allow.reshape(frames * frames, rows, 1).astype(f32), (frames * frames, rows, 128)
    )
    own, sums = send_back(attention(pay_at, allow), cols_at)
    grad_out, grad_qkv = sums[:, :width], sums[:, width:]
    own = own.reshape(band, wide)
    results = [own[:, t * BLOCK : (t + 1) * BLOCK] for t in range(3)]
    zero = jnp.zeros((), bf16)

    def project_back(a, t):
        return lax.dot_general(a, weights[t], (((1,), (1,)), ((), ())), preferred_element_type=f32)

    d_hidden = lax.optimization_barrier(
        (
            project_back(jnp.where(is_attn, zero, results[0]), 0)
            + project_back(results[1], 1)
            + project_back(results[2], 2)
        ).astype(bf16)
    )
    mixed = (tok_float + project_back(jnp.where(is_attn, results[0], zero), 0)).astype(bf16)
    grad = d_hidden.astype(f32) * norm_gain
    grad_tokens = cotangent.astype(f32) + inv_rms * (
        grad - normed * jnp.mean(grad * normed, -1, keepdims=True)
    )
    return (mixed[None], grad_tokens.astype(bf16)[None], grad_qkv, grad_out)


def solution(mesh):
    placed = (
        P("groups", "tm", None),
        P(),
        P("tm", None),
        P("tm", None),
        P("groups", None, None),
        P("groups", "tm"),
        P("groups", "tm", None),
    )
    small = mesh.shape["tm"] == FRAMES_HERE * SPLIT and mesh.shape["groups"] == 2
    return jax.shard_map(
        four_frames if small else per_device,
        mesh=mesh,
        in_specs=placed,
        out_specs=(
            P("groups", "tm", None),
            P("groups", "tm", None),
            P(("groups", "tm"), None),
            P(("groups", "tm"), None),
        ),
        check_vma=False,
    )
```

```python
import functools

import jax
import jax.numpy as jnp
from jax import lax
from jax.experimental import pallas as pl
from jax.experimental.pallas import tpu as pltpu
from jax.sharding import PartitionSpec as P

HD = 72
SPLIT = 4
TB = 2
TILE = 16


EPS = 1e-06
FRAMES_HERE = 4
BLOCK = 768
MESH = pl.DeviceIdType.MESH


def temporal(qkv_cols, dattn_cols, keep_cols, block_mask, frames):
    videos, per_owner, owners, _ = qkv_cols.shape
    band_count = owners // frames
    heads_n = dattn_cols.shape[-1] // HD
    scale = HD ** (-0.5)
    parts = qkv_cols.reshape(videos, per_owner, frames, band_count, 3, heads_n, HD)
    queries = parts[:, :, :, :, 0]
    key_part = parts[:, :, :, :, 1]
    val_part = parts[:, :, :, :, 2]
    d_out = dattn_cols.reshape(videos, per_owner, frames, band_count, heads_n, HD)
    frame_block = jnp.arange(frames) // TB
    blocks = jnp.repeat(jnp.repeat(block_mask, TB, 1), TB, 2) > 0
    same_block = frame_block[:, None] == frame_block[None, :]
    block_allow = blocks | same_block[None]
    kept = jnp.transpose(keep_cols.reshape(videos, per_owner, frames, band_count) > 0, (0, 1, 3, 2))
    diag_one = jnp.arange(frames)[:, None] == jnp.arange(frames)[None, :]
    allow = block_allow[:, None, None, None, :, :] & (kept[:, :, :, None, None, :] | diag_one)
    scores = (
        jnp.einsum("vrfshd,vrgshd->vrshfg", queries, key_part, preferred_element_type=jnp.float32)
        * scale
    )
    scores = jnp.where(allow, scores, -1e30)
    row_top = jnp.max(scores, -1, keepdims=True)
    expo = jnp.exp(scores - row_top)
    probs = expo / jnp.sum(expo, -1, keepdims=True)
    probs_b = probs.astype(jnp.bfloat16)
    attn = jnp.einsum(
        "vrshfg,vrgshd->vrfshd", probs_b, val_part, preferred_element_type=jnp.float32
    ).astype(jnp.bfloat16)
    dprob = jnp.einsum("vrfshd,vrgshd->vrshfg", d_out, val_part, preferred_element_type=jnp.float32)
    dscore = probs * (dprob - jnp.sum(probs * dprob, -1, keepdims=True))
    dscore_b = dscore.astype(jnp.bfloat16)
    grad_query = (
        jnp.einsum("vrshfg,vrgshd->vrfshd", dscore_b, key_part, preferred_element_type=jnp.float32)
        * scale
    ).astype(jnp.bfloat16)
    grad_key = (
        jnp.einsum("vrshfg,vrfshd->vrgshd", dscore_b, queries, preferred_element_type=jnp.float32)
        * scale
    ).astype(jnp.bfloat16)
    grad_value = jnp.einsum(
        "vrshfg,vrfshd->vrgshd", probs_b, d_out, preferred_element_type=jnp.float32
    ).astype(jnp.bfloat16)
    d_qkv = jnp.stack([grad_query, grad_key, grad_value], axis=4).reshape(
        videos, per_owner, owners, -1
    )
    return (attn.reshape(videos, per_owner, owners, -1), d_qkv)


def per_device(tokens, norm_gain, w_qkv, w_out, block_mask, keep_tiles, cotangent):
    owners = lax.axis_size("tm")
    videos, band_len, model_width = tokens.shape
    per_owner = band_len // owners
    frames = owners // SPLIT
    qkv_full, out_full = (
        lax.all_gather(w_qkv, "tm", axis=0, tiled=True),
        lax.all_gather(w_out, "tm", axis=0, tiled=True),
    )
    tok_float = tokens.astype(jnp.float32)
    inv_rms = lax.rsqrt(jnp.mean(tok_float * tok_float, -1, keepdims=True) + EPS)
    normed = tok_float * inv_rms
    hidden = (normed * norm_gain).astype(jnp.bfloat16)
    keep_tok = jnp.repeat(keep_tiles, TILE, axis=1).reshape(videos, per_owner, owners)
    qkv = jnp.dot(hidden, qkv_full, preferred_element_type=jnp.float32).astype(jnp.bfloat16)
    d_attn = jnp.dot(cotangent, out_full, preferred_element_type=jnp.float32).astype(jnp.bfloat16)
    qkv_cols, dattn_cols, keep_cols = (
        lax.all_to_all(
            qkv.reshape(videos, per_owner, owners, -1),
            "tm",
            split_axis=2,
            concat_axis=2,
            tiled=True,
        ),
        lax.all_to_all(
            d_attn.reshape(videos, per_owner, owners, -1),
            "tm",
            split_axis=2,
            concat_axis=2,
            tiled=True,
        ),
        lax.all_to_all(keep_tok, "tm", split_axis=2, concat_axis=2, tiled=True),
    )
    attn_cols, dqkv_cols = temporal(qkv_cols, dattn_cols, keep_cols, block_mask, frames)
    attn_rows, dqkv_rows = (
        lax.all_to_all(attn_cols, "tm", split_axis=2, concat_axis=2, tiled=True),
        lax.all_to_all(dqkv_cols, "tm", split_axis=2, concat_axis=2, tiled=True),
    )
    attn = attn_rows.reshape(videos, band_len, -1)
    d_qkv = dqkv_rows.reshape(videos, band_len, -1)
    part_qkv = jnp.einsum("vtd,vte->de", hidden, d_qkv, preferred_element_type=jnp.float32)
    part_out = jnp.einsum("vtd,vte->de", cotangent, attn, preferred_element_type=jnp.float32)
    d_hidden = lax.optimization_barrier(
        jnp.einsum("vte,de->vtd", d_qkv, qkv_full, preferred_element_type=jnp.float32).astype(
            jnp.bfloat16
        )
    )
    grad_qkv, grad_out = (
        lax.psum_scatter(part_qkv, "tm", scatter_dimension=0, tiled=True),
        lax.psum_scatter(part_out, "tm", scatter_dimension=0, tiled=True),
    )
    mixed = (
        tok_float + jnp.einsum("vte,de->vtd", attn, out_full, preferred_element_type=jnp.float32)
    ).astype(jnp.bfloat16)
    grad = d_hidden.astype(jnp.float32) * norm_gain
    grad_tokens = cotangent.astype(jnp.float32) + inv_rms * (
        grad - normed * jnp.mean(grad * normed, -1, keepdims=True)
    )
    return (mixed, grad_tokens.astype(jnp.bfloat16), grad_qkv, grad_out)


def pid(x):
    return {"tm": x}


def place():
    me = lax.axis_index("tm")
    z, b = me // SPLIT, me % SPLIT
    return me, z, b, b // 2, b % 2


def greet(peers):
    barrier = pltpu.get_barrier_semaphore()
    for peer in peers:
        pl.semaphore_signal(barrier, inc=1, device_id=peer, device_id_type=MESH)
    pl.semaphore_wait(barrier, len(peers))


def remote(src, dst, send_sem, recv_sem, peer):
    return pltpu.make_async_remote_copy(
        src_ref=src,
        dst_ref=dst,
        send_sem=send_sem,
        recv_sem=recv_sem,
        device_id=peer,
        device_id_type=MESH,
    )


def forward_kernel(
    w_ref, cols, keep, w_out, pay_out, keep_out, cols_out, held, left, pay,
    local_sem, send_z, send_y, send_x, send_c, recv, save_sem,
    send_k, recv_k, send_b, recv_b, send_p, recv_p, own_sem,
):
    f32 = jnp.float32
    x = lax.axis_index("groups")
    me, z, b, y, c = place()
    over_z = [pid((z + dz) % FRAMES_HERE * SPLIT + b) for dz in range(1, FRAMES_HERE)]
    over_b = [pid(z * SPLIT + (b + db) % SPLIT) for db in range(1, SPLIT)]
    over_y = pid(z * SPLIT + (1 - y) * 2 + c)
    over_c = pid(z * SPLIT + y * 2 + (1 - c))
    over_x = {"groups": 1 - x}
    greet(over_z + over_b + [over_x])
    blocks = (2, x, 1 - x)
    started = []

    def start(copy):
        copy.start()
        started.append(copy)

    def send(src, t, k, sem, peer):
        start(remote(src, held.at[t, k], sem, recv.at[t, k], peer))

    def arrived(t, k):
        remote(held.at[t, k], held.at[t, k], send_z.at[0, 0], recv.at[t, k], over_y).wait_recv()

    local = [
        pltpu.make_async_copy(w_ref.at[2], held.at[2, me], local_sem.at[0]),
        pltpu.make_async_copy(w_ref.at[x], held.at[x, me], local_sem.at[1]),
        pltpu.make_async_copy(cols, left, local_sem.at[2]),
        pltpu.make_async_copy(keep.at[z], keep_out.at[z], local_sem.at[3]),
        pltpu.make_async_copy(cols.at[b], cols_out.at[b], local_sem.at[4]),
    ]
    for copy in local:
        copy.start()
    for i in range(2):
        for dz in (2, 1, 3):
            send(w_ref.at[blocks[i]], blocks[i], me, send_z.at[i, dz], over_z[dz - 1])
    shards = [(z + FRAMES_HERE - dz) % FRAMES_HERE * SPLIT for dz in range(FRAMES_HERE)]
    order = [0, 1, 3, 2]

    def from_z(i):
        t = blocks[i]
        for dz in order:
            k = shards[dz] + b
            if dz:
                arrived(t, k)
            src = held.at[t, k] if dz else w_ref.at[t]
            send(src, t, k, send_y.at[i, dz], over_y)
            if i == 1:
                send(src, t, k, send_x.at[0, dz], over_x)
            send(src, t, k, send_c.at[i, 0, dz], over_c)

    def from_y(i):
        t = blocks[i]
        for dz in order:
            k = shards[dz] + (1 - y) * 2 + c
            arrived(t, k)
            if i == 1:
                send(held.at[t, k], t, k, send_x.at[1, dz], over_x)
            send(held.at[t, k], t, k, send_c.at[i, 1, dz], over_c)

    def from_x(j):
        t = blocks[2]
        for dz in order:
            k = shards[dz] + (y if j == 0 else 1 - y) * 2 + c
            arrived(t, k)
            send(held.at[t, k], t, k, send_c.at[2, j, dz], over_c)

    rows = pay.shape[2]
    width = 3 * BLOCK // 4
    own = []

    def project(i):
        t = blocks[i]
        for yy in range(2):
            for zz in range(FRAMES_HERE):
                arrived(t, zz * SPLIT + yy * 2 + (1 - c))
        save = pltpu.make_async_copy(held.at[t], w_out.at[t], save_sem.at[i])
        save.start()
        own.append(save)

        def over_shards(kind):
            total = None
            for k in range(FRAMES_HERE * SPLIT):
                term = lax.dot_general(
                    left[k % SPLIT, kind, k // SPLIT],
                    held[t, k],
                    (((0,), (0,)), ((), ())),
                    preferred_element_type=f32,
                )
                total = term if total is None else total + term
            return total

        def store(value):
            value = value.astype(pay.dtype)
            for to in range(FRAMES_HERE):
                pay[t, to] = value[to * rows : (to + 1) * rows]

        if i == 0:
            store(over_shards(0))
        else:

            @pl.when(t != 0)
            def _():
                store(over_shards(0))

            @pl.when(t == 0)
            def _():
                value = over_shards(0)
                lane = lax.broadcasted_iota(jnp.int32, value.shape, 1)
                store(jnp.where(lane < width, over_shards(1), value))

        lanes = pl.ds(pl.multiple_of(t * BLOCK, BLOCK), BLOCK)
        for dz in (2, 1, 3):
            start(
                remote(
                    pay.at[t, (z + dz) % FRAMES_HERE],
                    pay_out.at[z, :, lanes],
                    send_p.at[i, dz],
                    recv_p.at[i, dz],
                    over_z[dz - 1],
                )
            )
        keep_own = pltpu.make_async_copy(pay.at[t, z], pay_out.at[z, :, lanes], own_sem.at[i])
        keep_own.start()
        own.append(keep_own)

    from_z(0)
    from_y(0)
    from_z(1)
    for copy in local:
        copy.wait()
    project(0)
    from_y(1)
    from_x(0)
    for dz in (2, 1, 3):
        to = (z + dz) % FRAMES_HERE
        start(
            remote(keep.at[to], keep_out.at[z], send_k.at[dz], recv_k.at[dz], over_z[dz - 1])
        )
    for db in (2, 1, 3):
        to = (b + db) % SPLIT
        start(remote(cols.at[to], cols_out.at[b], send_b.at[db], recv_b.at[db], over_b[db - 1]))
    project(1)
    from_x(1)
    project(2)
    for dz in (1, 2, 3):
        came = (z + FRAMES_HERE - dz) % FRAMES_HERE
        peer = over_z[dz - 1]
        remote(keep.at[z], keep_out.at[came], send_k.at[dz], recv_k.at[dz], peer).wait_recv()
        for i in range(3):
            lanes = pl.ds(pl.multiple_of(blocks[i] * BLOCK, BLOCK), BLOCK)
            remote(
                pay.at[blocks[i], z],
                pay_out.at[came, :, lanes],
                send_p.at[i, dz],
                recv_p.at[i, dz],
                peer,
            ).wait_recv()
    for db in (1, 2, 3):
        came = (b + SPLIT - db) % SPLIT
        remote(cols.at[b], cols_out.at[came], send_b.at[db], recv_b.at[db], over_b[db - 1]).wait_recv()
    for copy in own:
        copy.wait()
    for copy in started:
        copy.wait_send()


def forward(blocks, cols, keep):
    owners = FRAMES_HERE * SPLIT
    dma = pltpu.SemaphoreType.DMA
    shard = blocks.shape[1]
    rows = cols.shape[-1] // FRAMES_HERE
    held = (3, owners, shard, BLOCK)
    pay = (FRAMES_HERE, rows, 3 * BLOCK)
    return pl.pallas_call(
        forward_kernel,
        out_shape=[
            jax.ShapeDtypeStruct(held, blocks.dtype),
            jax.ShapeDtypeStruct(pay, blocks.dtype),
            jax.ShapeDtypeStruct(keep.shape, keep.dtype),
            jax.ShapeDtypeStruct(cols.shape, cols.dtype),
        ],
        in_specs=[pl.BlockSpec(memory_space=pl.ANY)] * 3,
        out_specs=[pl.BlockSpec(memory_space=pl.ANY)] * 4,
        scratch_shapes=[
            pltpu.VMEM(held, blocks.dtype),
            pltpu.VMEM(cols.shape, cols.dtype),
            pltpu.VMEM((3, FRAMES_HERE, rows, BLOCK), blocks.dtype),
            dma((5,)),
            dma((2, 4)),
            dma((2, 4)),
            dma((2, 4)),
            dma((3, 2, 4)),
            dma((3, owners)),
            dma((3,)),
            dma((4,)),
            dma((4,)),
            dma((4,)),
            dma((4,)),
            dma((3, 4)),
            dma((3, 4)),
            dma((3,)),
        ],
        compiler_params=pltpu.CompilerParams(
            collective_id=0, has_side_effects=True, vmem_limit_bytes=40 * 1024 * 1024
        ),
    )(blocks, cols, keep)


def back_kernel(
    res, cols, own, sums, tok, left, part, came, extra,
    local_sem, send_z, send_y, send_c, recv, own_sem, send_p, recv_p, recv_x,
):
    f32, bf16 = jnp.float32, jnp.bfloat16
    me, z, b, y, c = place()
    over_z = [pid((z + dz) % FRAMES_HERE * SPLIT + b) for dz in range(1, FRAMES_HERE)]
    over_y = pid(z * SPLIT + (1 - y) * 2 + c)
    over_c = pid(z * SPLIT + y * 2 + (1 - c))
    greet(over_z + [over_y, over_c])
    block = BLOCK // 2
    started = []
    width = res.shape[-1] // 4

    def lanes(t):
        return pl.ds(t * block, block)

    def send(src, t, i, j, sem, peer):
        slot = i * FRAMES_HERE + j
        copy = remote(src, tok.at[slot, :, lanes(t)], sem, recv.at[t, slot], peer)
        copy.start()
        started.append(copy)

    def arrived(t, i, j):
        slot = i * FRAMES_HERE + j
        place_at = tok.at[slot, :, lanes(t)]
        remote(place_at, place_at, send_z.at[0, 0], recv.at[t, slot], over_y).wait_recv()

    for t in range(6):
        for dz in (2, 1, 3):
            send(
                res.at[(z + dz) % FRAMES_HERE, :, lanes(t)],
                t, b, z, send_z.at[t, dz], over_z[dz - 1],
            )
    local = [
        pltpu.make_async_copy(res.at[z], tok.at[b * FRAMES_HERE + z], local_sem.at[0]),
        pltpu.make_async_copy(cols, left, local_sem.at[1]),
    ]
    for copy in local:
        copy.start()
    order = [0, 1, 3, 2]

    def from_z(t):
        for dz in order:
            j = (z + FRAMES_HERE - dz) % FRAMES_HERE
            if dz:
                arrived(t, b, j)
                src = tok.at[b * FRAMES_HERE + j, :, lanes(t)]
            else:
                src = res.at[z, :, lanes(t)]
            send(src, t, b, j, send_y.at[t, dz], over_y)
            send(src, t, b, j, send_c.at[t, 0, dz], over_c)

    def from_y(t):
        for dz in order:
            i, j = (1 - y) * 2 + c, (z + FRAMES_HERE - dz) % FRAMES_HERE
            arrived(t, i, j)
            src = tok.at[i * FRAMES_HERE + j, :, lanes(t)]
            send(src, t, i, j, send_c.at[t, 1, dz], over_c)

    def from_c(t):
        for yy in range(2):
            for j in range(FRAMES_HERE):
                arrived(t, yy * 2 + (1 - c), j)

    low = z < 2
    end = (z == 0) | (z == 3)

    def at(m):
        return jnp.where(low, m, 3 - m)

    def block_copy(t, owner, peer_z, to_extra):
        src = part.at[owner, :, lanes(t)]
        peer = pid(peer_z * SPLIT + b)
        if to_extra:
            return remote(src, extra.at[t], send_p.at[t, 2], recv_x.at[t], peer)
        return remote(src, came.at[t, z], send_p.at[t, 2], recv_p.at[t, z], peer)

    def near_copy(t, which):
        owner = jnp.where(end, at(1 + which), at(2 * which))
        src = part.at[owner, :, lanes(t)]
        peer = pid(owner * SPLIT + b)
        return remote(src, came.at[t, z], send_p.at[t, which], recv_p.at[t, z], peer)

    def contract(t):
        right = tok[:, :, lanes(t)].reshape(SPLIT, FRAMES_HERE * tok.shape[1], block)

        def over_tokens(kind):
            total = jnp.dot(left[0, kind], right[0], preferred_element_type=f32)
            for i in range(1, SPLIT):
                total += jnp.dot(left[i, kind], right[i], preferred_element_type=f32)
            return total

        product = over_tokens(1 if (t + 1) * block <= width else 0)
        if t * block < width < (t + 1) * block:
            lane = lax.broadcasted_iota(jnp.int32, product.shape, 1)
            product = jnp.where(lane < width - t * block, over_tokens(1), product)
        rows = part.shape[1]
        for owner in range(FRAMES_HERE):
            part[owner, :, t * block : (t + 1) * block] = product[owner * rows : (owner + 1) * rows]

        @pl.when(end)
        def _():
            block_copy(t, at(3), at(1), True).start()

        near_copy(t, 1).start()
        near_copy(t, 0).start()

    def pass_on(t):
        @pl.when(jnp.logical_not(end))
        def _():
            remote(extra.at[t], extra.at[t], send_p.at[t, 2], recv_x.at[t], over_y).wait_recv()
            far = at(3)
            part[far, :, t * block : (t + 1) * block] += extra[t]
            block_copy(t, far, far, False).start()

    from_z(0)
    from_y(0)
    from_z(1)
    for copy in local:
        copy.wait()
    mine = pltpu.make_async_copy(tok.at[pl.ds(b * FRAMES_HERE, FRAMES_HERE)], own, own_sem)
    for t in range(6):
        from_c(t)
        contract(t)
        if t < 5:
            from_y(t + 1)
        if t < 4:
            from_z(t + 2)
        if t == 4:
            mine.start()
        if t > 0:
            pass_on(t - 1)
    pass_on(5)

    def landed(t, src):
        remote(
            came.at[t, src], came.at[t, src], send_p.at[t, 0], recv_p.at[t, src], over_y
        ).wait_recv()

    for t in range(6):
        here = slice(t * block, (t + 1) * block)

        @pl.when(end)
        def _():
            landed(t, at(1))
            landed(t, at(2))
            sums[:, here] = part[z, :, here] + came[t, at(1)] + came[t, at(2)]

        @pl.when(jnp.logical_not(end))
        def _():
            landed(t, at(0))
            landed(t, at(2))
            landed(t, at(3))
            sums[:, here] = (part[z, :, here] + came[t, at(0)]) + (came[t, at(2)] + came[t, at(3)])

    mine.wait()
    for copy in started:
        copy.wait_send()
    for t in range(6):
        near_copy(t, 0).wait_send()
        near_copy(t, 1).wait_send()

        @pl.when(end)
        def _():
            block_copy(t, at(3), at(1), True).wait_send()

        @pl.when(jnp.logical_not(end))
        def _():
            block_copy(t, at(3), at(3), False).wait_send()


def send_back(res, cols):
    dma = pltpu.SemaphoreType.DMA
    frames, rows, wide = res.shape
    shard = cols.shape[2] // frames
    f32 = jnp.float32
    flops = 2 * cols.shape[2] * SPLIT * cols.shape[3] * wide
    return pl.pallas_call(
        back_kernel,
        out_shape=[
            jax.ShapeDtypeStruct(res.shape, res.dtype),
            jax.ShapeDtypeStruct((shard, wide), f32),
        ],
        in_specs=[pl.BlockSpec(memory_space=pl.ANY)] * 2,
        out_specs=[
            pl.BlockSpec(memory_space=pl.ANY),
            pl.BlockSpec(memory_space=pltpu.VMEM),
        ],
        scratch_shapes=[
            pltpu.VMEM((SPLIT * frames, rows, wide), res.dtype),
            pltpu.VMEM(cols.shape, cols.dtype),
            pltpu.VMEM((frames, shard, wide), f32),
            pltpu.VMEM((6, frames, shard, wide // 6), f32),
            pltpu.VMEM((6, shard, wide // 6), f32),
            dma((2,)),
            dma((6, 4)),
            dma((6, 4)),
            dma((6, 2, 4)),
            dma((6, 16)),
            dma,
            dma((6, 3)),
            dma((6, 4)),
            dma((6,)),
        ],
        cost_estimate=pl.CostEstimate(flops=flops, bytes_accessed=4 * res.size, transcendentals=0),
        compiler_params=pltpu.CompilerParams(
            collective_id=2, has_side_effects=True, vmem_limit_bytes=40 * 1024 * 1024
        ),
    )(res, cols)


def attention_kernel(pay, allow, out, dk_sum, dv_sum):
    f32, bf16 = jnp.float32, jnp.bfloat16
    width = pay.shape[-1] // 4
    rows = pay.shape[1]
    scale = HD ** (-0.5)
    frames = pay.shape[0]
    row = lax.broadcasted_iota(jnp.int32, (width, 128), 0)
    lane = lax.broadcasted_iota(jnp.int32, (width, 128), 1)
    gather = ((row >= lane * HD) & (row < lane * HD + HD)).astype(f32).astype(bf16)
    row_t = lax.broadcasted_iota(jnp.int32, (128, width), 1)
    lane_t = lax.broadcasted_iota(jnp.int32, (128, width), 0)
    spread = ((row_t >= lane_t * HD) & (row_t < lane_t * HD + HD)).astype(f32).astype(bf16)

    def part(i, f):
        return pay[f, :, i * width : (i + 1) * width].astype(f32)

    def head_sums(prod):
        high = prod.astype(bf16)
        low = (prod - high.astype(f32)).astype(bf16)
        return jnp.dot(high, gather, preferred_element_type=f32) + jnp.dot(
            low, gather, preferred_element_type=f32
        )

    for f in range(frames):
        query, d_out = part(1, f), part(0, f)
        scores, dprob = [], []
        for g in range(frames):
            raw = head_sums(query * part(2, g)) * scale
            scores.append(jnp.where(allow[f * frames + g] > 0, raw, -1e30))
            dprob.append(head_sums(d_out * part(3, g)))
        top = functools.reduce(jnp.maximum, scores)
        expo = [jnp.exp(s - top) for s in scores]
        total = functools.reduce(jnp.add, expo)
        probs = [e / total for e in expo]
        inner = functools.reduce(jnp.add, [p * d for p, d in zip(probs, dprob)])
        attn = jnp.zeros((rows, width), f32)
        d_query = jnp.zeros((rows, width), f32)
        for g in range(frames):
            pb = jnp.dot(probs[g].astype(bf16), spread, preferred_element_type=f32)
            dscore = (probs[g] * (dprob[g] - inner)).astype(bf16)
            ds = jnp.dot(dscore, spread, preferred_element_type=f32)
            attn += pb * part(3, g)
            d_query += ds * part(2, g)
            if f == 0:
                dk_sum[g] = ds * query
                dv_sum[g] = pb * d_out
            else:
                dk_sum[g] += ds * query
                dv_sum[g] += pb * d_out
        out[f, :, 0:width] = attn.astype(bf16)
        out[f, :, width : 2 * width] = (d_query * scale).astype(bf16)
    for g in range(frames):
        out[g, :, 2 * width : 3 * width] = (dk_sum[g] * scale).astype(bf16)
        out[g, :, 3 * width : 4 * width] = dv_sum[g].astype(bf16)


def attention(pay, allow):
    frames, rows, wide = pay.shape
    return pl.pallas_call(
        attention_kernel,
        out_shape=jax.ShapeDtypeStruct(pay.shape, pay.dtype),
        in_specs=[pl.BlockSpec(memory_space=pltpu.VMEM)] * 2,
        out_specs=pl.BlockSpec(memory_space=pltpu.VMEM),
        scratch_shapes=[pltpu.VMEM((frames, rows, wide // 4), jnp.float32)] * 2,
        compiler_params=pltpu.CompilerParams(vmem_limit_bytes=32 * 1024 * 1024),
    )(pay, allow)


def four_frames(tokens, norm_gain, w_qkv, w_out, block_mask, keep_tiles, cotangent):
    f32, bf16 = jnp.float32, jnp.bfloat16
    frames = FRAMES_HERE
    tokens, cotangent = tokens[0], cotangent[0]
    band, model = tokens.shape
    shard, wide_qkv = w_qkv.shape
    wide = wide_qkv + w_out.shape[1]
    rows = band // frames
    width = wide // 4
    blocks = jnp.concatenate([w_out, w_qkv], 1).reshape(shard, 3, BLOCK).transpose(1, 0, 2)
    tok_float = tokens.astype(f32)
    inv_rms = lax.rsqrt(jnp.mean(tok_float * tok_float, -1, keepdims=True) + EPS)
    normed = tok_float * inv_rms
    hidden = (normed * norm_gain).astype(bf16)
    is_attn = jnp.arange(BLOCK) < width
    keep = jnp.repeat(keep_tiles[0].astype(f32), TILE).reshape(frames, 1, rows)
    keep = jnp.pad(jnp.broadcast_to(keep, (frames, 8, rows)), ((0, 0), (0, 0), (0, 128 - rows)))

    def owners_columns(a):
        cut = a.T.reshape(frames, SPLIT, shard, band)
        return cut.transpose(1, 0, 2, 3)[:, None]

    cols = jnp.concatenate([owners_columns(hidden), owners_columns(cotangent)], 1)
    gathered, pay_at, keep_at, cols_at = forward(blocks, cols, keep)
    weights = [gathered[t].reshape(model, BLOCK) for t in range(3)]
    cols_at = cols_at.reshape(SPLIT, 2, frames * shard, band)

    frame_block = jnp.arange(frames) // TB
    same_block = frame_block[:, None] == frame_block[None, :]
    seen = (jnp.repeat(jnp.repeat(block_mask[0], TB, 0), TB, 1) > 0) | same_block
    diag_one = jnp.arange(frames)[:, None] == jnp.arange(frames)[None, :]
    kept = keep_at[:, 0, :rows] > 0
    allow = seen[:, :, None] & (kept[None] | diag_one[:, :, None])
    allow = jnp.broadcast_to(
        allow.reshape(frames * frames, rows, 1).astype(f32), (frames * frames, rows, 128)
    )
    own, sums = send_back(attention(pay_at, allow), cols_at)
    grad_out, grad_qkv = sums[:, :width], sums[:, width:]
    own = own.reshape(band, wide)
    results = [own[:, t * BLOCK : (t + 1) * BLOCK] for t in range(3)]
    zero = jnp.zeros((), bf16)

    def project_back(a, t):
        return lax.dot_general(a, weights[t], (((1,), (1,)), ((), ())), preferred_element_type=f32)

    d_hidden = lax.optimization_barrier(
        (
            project_back(jnp.where(is_attn, zero, results[0]), 0)
            + project_back(results[1], 1)
            + project_back(results[2], 2)
        ).astype(bf16)
    )
    mixed = (tok_float + project_back(jnp.where(is_attn, results[0], zero), 0)).astype(bf16)
    grad = d_hidden.astype(f32) * norm_gain
    grad_tokens = cotangent.astype(f32) + inv_rms * (
        grad - normed * jnp.mean(grad * normed, -1, keepdims=True)
    )
    return (mixed[None], grad_tokens.astype(bf16)[None], grad_qkv, grad_out)


def solution(mesh):
    placed = (
        P("groups", "tm", None),
        P(),
        P("tm", None),
        P("tm", None),
        P("groups", None, None),
        P("groups", "tm"),
        P("groups", "tm", None),
    )
    small = mesh.shape["tm"] == FRAMES_HERE * SPLIT and mesh.shape["groups"] == 2
    return jax.shard_map(
        four_frames if small else per_device,
        mesh=mesh,
        in_specs=placed,
        out_specs=(
            P("groups", "tm", None),
            P("groups", "tm", None),
            P(("groups", "tm"), None),
            P(("groups", "tm"), None),
        ),
        check_vma=False,
    )
```
